32 devices in a mesh: lon: 4 (over z), batch: 8 (over y, x, core).
Axes of the slice: x: 2, y: 2, z: 4, core: 2. Of those that a mesh axis runs over, the one named last changes fastest.
Arguments:
- inputs: float32 [64, 32, 32, 128], P('batch', None, 'lon'), may hold values from -21 to 21
- weight_one: float32 [3, 3, 128, 128], replicated, may hold values from -0.1875 to 0.1875
- bias_one: float32 [128], replicated, may hold values from -3 to 3
- first_norm_scale: float32 [128], replicated, may hold values from 0.1 to 1.9
- first_norm_bias: float32 [128], replicated, may hold values from -3 to 3
- weight_two: float32 [3, 3, 128, 128], replicated, may hold values from -0.1875 to 0.1875
- bias_two: float32 [128], replicated, may hold values from -3 to 3
- second_norm_scale: float32 [128], replicated, may hold values from 0.1 to 1.9
- second_norm_bias: float32 [128], replicated, may hold values from -3 to 3
- cotangent: float32 [64, 32, 32, 128], P('batch', None, 'lon'), may hold values from -6 to 6
Outputs:
- block_output: float32 [64, 32, 32, 128], P('batch', None, 'lon')
- input_grad: float32 [64, 32, 32, 128], P('batch', None, 'lon')
- weight_one_grad: float32 [3, 3, 128, 128], replicated
- bias_one_grad: float32 [128], replicated
- gain_one_grad: float32 [128], replicated
- shift_one_grad: float32 [128], replicated
- weight_two_grad: float32 [3, 3, 128, 128], replicated
- bias_two_grad: float32 [128], replicated
- gain_two_grad: float32 [128], replicated
- shift_two_grad: float32 [128], replicated
The draws below stay inside these ranges and needn't reach their ends.
All inputs are finite; a program needn't handle non-finite values.
Results may differ from the reference program's by a relative error of at most 0.018.
Values may be sent and summed in bfloat16 or wider, within the bound.
A program may use at most 64 MiB of HBM per device.

```python
import jax
import jax.numpy as jnp
from jax import lax

C = 128
LAT = 32
LON = 32
BATCH = 64


def draw_inputs(key, part):
    key = jax.random.fold_in(key, 11)
    third = jax.random.fold_in(key, 2)
    sample_pos = jnp.arange(BATCH, dtype=jnp.float32) / max(BATCH - 1, 1)
    column_pos = jnp.arange(LON, dtype=jnp.float32) / max(LON - 1, 1)
    scale = jnp.exp(jnp.log(3.0) * (sample_pos[:, None, None, None] + column_pos[None, None, :, None])) / 3.0
    values = jnp.clip(jax.random.normal(third, (BATCH, LAT, LON, C), jnp.float32), -6.0, 6.0) * scale
    return values.astype(jnp.float32)


def levels(stream_key, extent, pieces, smallest, largest):
    factor_of, own = 1.0, jax.random.fold_in(stream_key, 6)
    for axis_at, blocks in pieces:
        draws = jnp.exp(jax.random.uniform(jax.random.fold_in(own, axis_at), (blocks,), jnp.float32, smallest / len(pieces), largest / len(pieces)))
        factor_of = factor_of * jnp.repeat(draws, extent[axis_at] // blocks).reshape([-1 if axis == axis_at else 1 for axis in range(len(extent))])
    return factor_of


def centred(own_key, dims, spread, limit, cuts=(), kind=jnp.bfloat16):
    entries = spread * jax.random.normal(own_key, dims, jnp.float32)
    if cuts:
        entries = entries * levels(own_key, dims, cuts, -0.22, 0.18)
    return jnp.clip(entries, -limit, limit).astype(kind)


def setup_inputs(seed: int = 0) -> dict:
    seeds = jax.random.split(jax.random.key(seed), 11)
    return {
        "inputs": draw_inputs(jax.random.fold_in(seeds[10], 71), 0),
        "weight_one": centred(seeds[1], (3, 3, C, C), (9 * C) ** -0.5, 0.1875, (), jnp.float32),
        "bias_one": centred(seeds[2], (C,), 0.5, 3.0, (), jnp.float32),
        "first_norm_scale": jnp.clip(1.0 + 0.18 * jax.random.normal(seeds[3], (C,), jnp.float32), 0.1, 1.9),
        "first_norm_bias": centred(seeds[4], (C,), 0.5, 3.0, (), jnp.float32),
        "weight_two": centred(seeds[5], (3, 3, C, C), (9 * C) ** -0.5, 0.1875, (), jnp.float32),
        "bias_two": centred(seeds[6], (C,), 0.5, 3.0, (), jnp.float32),
        "second_norm_scale": jnp.clip(1.0 + 0.18 * jax.random.normal(seeds[7], (C,), jnp.float32), 0.1, 1.9),
        "second_norm_bias": centred(seeds[8], (C,), 0.5, 3.0, (), jnp.float32),
        "cotangent": centred(seeds[9], (BATCH, LAT, LON, C), 1.0, 6.0, ((0, 8), (2, 4)), jnp.float32),
    }


@jax.custom_vjp
def low(v):
    return lax.optimization_barrier(v.astype(jnp.bfloat16)).astype(jnp.float32)

@jax.custom_vjp
def low_back(v):
    return v

def low_keep(v):
    return (low(v), None)

def low_pass(kept, upstream_gradient):
    return (upstream_gradient,)

def back_keep(v):
    return (v, None)

def back_low(kept, upstream_gradient):
    return (low(upstream_gradient),)
low.defvjp(low_keep, low_pass)
low_back.defvjp(back_keep, back_low)

def convolve(field, kernel):
    padded = jnp.pad(field, ((0, 0), (0, 0), (1, 1), (0, 0)), mode='wrap')
    return lax.conv_general_dilated(padded, kernel, (1, 1), ((1, 1), (0, 0)), dimension_numbers=('NHWC', 'HWIO', 'NHWC'), precision=lax.Precision.HIGHEST)

def batch_norm(act, norm_scale, norm_bias):
    mean = lax.optimization_barrier(jnp.mean(act, axis=(0, 1, 2)))
    dev = act - mean
    var = lax.optimization_barrier(jnp.mean(dev * dev, axis=(0, 1, 2)))
    return dev * lax.rsqrt(var + 1e-05) * norm_scale + norm_bias

def forward(inputs, weight_one, bias_one, first_norm_scale, first_norm_bias, weight_two, bias_two, second_norm_scale, second_norm_bias):
    first_conv_output = low_back(convolve(low(inputs), low(weight_one)) + bias_one)
    first_norm_output = batch_norm(jax.nn.silu(first_conv_output), first_norm_scale, first_norm_bias)
    second_conv_output = low_back(convolve(low(first_norm_output), low(weight_two)) + bias_two)
    second_norm_output = batch_norm(jax.nn.silu(second_conv_output), second_norm_scale, second_norm_bias)
    return inputs + second_norm_output

def reference(inputs, weight_one, bias_one, first_norm_scale, first_norm_bias, weight_two, bias_two, second_norm_scale, second_norm_bias, cotangent):
    result, pullback = jax.vjp(forward, inputs, weight_one, bias_one, first_norm_scale, first_norm_bias, weight_two, bias_two, second_norm_scale, second_norm_bias)
    grads = pullback(cotangent)
    return (result, grads[0], grads[1], grads[2], grads[3], grads[4], grads[5], grads[6], grads[7], grads[8])
```

```python
import functools

import jax
import jax.numpy as jnp
from jax import lax
from jax.experimental import pallas as pl
from jax.experimental.pallas import tpu as pltpu
from jax.sharding import PartitionSpec as P

MESH = pl.DeviceIdType.MESH
F32, BF16 = jnp.float32, jnp.bfloat16
VMEM = pltpu.VMEM
DMA = pltpu.SemaphoreType.DMA

H_X, H_COT, H_Z1, H_Z2, H_D = range(5)
R_A, R_B, R_C, R_W2 = range(4)
B1, G1, S1, B2, G2, S2 = range(6)


def twice(row):
    return jnp.concatenate([row, row], axis=-1)


def silu_parts(pre):
    sig = 0.5 * jnp.tanh(0.5 * pre) + 0.5
    return pre * sig, sig * (1.0 + pre * (1.0 - sig))


def owners_of(chips, tiles):
    for size in range(1, tiles + 1):
        if tiles % size == 0 and tiles // size <= chips:
            return tiles // size, size


def main_kernel(n_lon, n_batch, x_hbm, cot_hbm, w1_hbm, w2_hbm, b1_hbm, g1_hbm, s1_hbm, b2_hbm, g2_hbm, s2_hbm,
                y_ref, ig_ref, wg1_ref, wg2_ref, vec_ref,
                xin, cot, w1f, w2f, par, vx, vn, vp, kc1, kc2, kd1, kd2, z1, a1, slope1, a2, slope2, dref, gbuf, gptg,
                hsend, hrecv, ar0, ar1, ar2, ar3, wsend, crecv, rsrc, rrecv, ag,
                load_sem, hs_sem, hr_sem, as_sem, ar_sem, cs_sem, cr_sem, rs_sem, rr_sem, gs_sem, gr_sem, fs_sem, fr_sem):
    samples, pairs, _, width, chan = x_hbm.shape
    lanes, cells = 2 * chan, width * samples
    rows = pairs * cells
    n_dev = n_lon * n_batch
    chips, plane = n_dev // 2, n_batch // 2
    local = 2.0 * rows
    total = local * n_dev
    n_own, own_rows = rsrc.shape[1], rsrc.shape[2]
    per_plane = -(-n_own // n_lon)
    half = wsend.shape[2]

    my_lon, my_batch = lax.axis_index("lon"), lax.axis_index("batch")
    me = my_lon * n_batch + my_batch
    core, my_place = my_batch % 2, my_batch // 2
    my_chip = my_lon * plane + my_place
    my_own = my_lon * per_plane + my_place
    is_own = jnp.logical_and(my_place < per_plane, my_own < n_own)
    sibling = (my_lon, my_batch + 1 - 2 * core)
    left = ((my_lon + n_lon - 1) % n_lon, my_batch)
    right = ((my_lon + 1) % n_lon, my_batch)

    def device(t):
        return (t // n_batch, t % n_batch)

    def to_device(src, dst, send, recv, where):
        return pltpu.make_async_remote_copy(src, dst, send, recv, device_id=where, device_id_type=MESH)

    def wait_bytes(ref, sem):
        pltpu.make_async_copy(ref, ref, sem).wait()

    def field_loads(src, dst, sem):
        return [
            pltpu.make_async_copy(src.at[b, :, s], dst.at[:, :, b, pl.ds(s * chan, chan)], sem)
            for b in range(samples)
            for s in range(2)
        ]

    for copy in field_loads(x_hbm, xin, load_sem.at[0]):
        copy.start()
    pltpu.make_async_copy(w1_hbm, w1f, load_sem.at[2]).start()
    for copy in field_loads(cot_hbm, cot, load_sem.at[1]):
        copy.start()
    pltpu.make_async_copy(w2_hbm, w2f, load_sem.at[3]).start()
    for i, src in enumerate((b1_hbm, g1_hbm, s1_hbm, b2_hbm, g2_hbm, s2_hbm)):
        pltpu.make_async_copy(src, par.at[i], load_sem.at[4]).start()

    barrier = pltpu.get_barrier_semaphore()
    for k in range(1, n_dev):
        pl.semaphore_signal(barrier, inc=1, device_id=device((me + k) % n_dev), device_id_type=MESH)

    def param(i):
        return par[i]

    def column(field, j):
        return field[:, j * samples:(j + 1) * samples, :]

    def halo_copies(kind):
        return (
            to_device(hsend.at[kind, 0], hrecv.at[kind, 1], hs_sem.at[kind, 0], hr_sem.at[kind, 1], left),
            to_device(hsend.at[kind, 1], hrecv.at[kind, 0], hs_sem.at[kind, 1], hr_sem.at[kind, 0], right),
        )

    def halo_put(kind, field):
        hsend[kind, 0] = column(field, 0).reshape(pairs * samples, lanes).astype(BF16)
        hsend[kind, 1] = column(field, width - 1).reshape(pairs * samples, lanes).astype(BF16)

    def halo_send(kind):
        for copy in halo_copies(kind):
            copy.start()

    def halo_wait(kind):
        for copy in halo_copies(kind):
            copy.wait_recv()

    def halo_get(kind):
        return [hrecv[kind, side].astype(F32).reshape(pairs, samples, lanes) for side in range(2)]

    def pack(ref, field, west, east):
        for s in range(2):
            part = field[:, :, s * chan:(s + 1) * chan]
            at = (slice(s, s + pairs), slice(None), slice((1 - s) * chan, (2 - s) * chan))
            ref[(1,) + at] = part.astype(BF16)
            lo = west[:, :, s * chan:(s + 1) * chan]
            hi = east[:, :, s * chan:(s + 1) * chan]
            ref[(0,) + at] = jnp.concatenate([lo, part[:, :-samples]], axis=1).astype(BF16)
            ref[(2,) + at] = jnp.concatenate([part[:, samples:], hi], axis=1).astype(BF16)

    def pack_inner(ref, field):
        for s in range(2):
            part = field[:, :, s * chan:(s + 1) * chan]
            rows_at, lanes_at = slice(s, s + pairs), slice((1 - s) * chan, (2 - s) * chan)
            ref[1, rows_at, :, lanes_at] = part.astype(BF16)
            ref[0, rows_at, 2 * samples:, lanes_at] = part[:, samples:-samples].astype(BF16)
            ref[2, rows_at, :cells - 2 * samples, lanes_at] = part[:, samples:-samples].astype(BF16)

    def pack_edges(ref, field_ref, west, east):
        first = field_ref[:, 0]
        last = field_ref[:, width - 1]
        for s in range(2):
            rows_at, lanes_at = slice(s, s + pairs), slice((1 - s) * chan, (2 - s) * chan)
            cut = slice(s * chan, (s + 1) * chan)
            ref[0, rows_at, :2 * samples, lanes_at] = jnp.concatenate([west[:, :, cut], first[:, :, cut]], axis=1).astype(BF16)
            ref[2, rows_at, cells - 2 * samples:, lanes_at] = jnp.concatenate([last[:, :, cut], east[:, :, cut]], axis=1).astype(BF16)

    def clear_pads(ref):
        for q in range(3):
            ref[q, 0, :, :chan] = jnp.zeros((cells, chan), BF16)
            ref[q, pairs, :, chan:] = jnp.zeros((cells, chan), BF16)

    def kernel_blocks(forward, backward, weight):
        none = jnp.zeros((chan, chan), BF16)
        for q in range(3):
            taps = [weight[pl.ds((p * 3 + q) * chan, chan), :].astype(BF16) for p in range(3)]
            turned = [tap.T for tap in taps]
            for t in range(4):
                for s in range(2):
                    p = t - s
                    there = 0 <= p <= 2
                    r, c = pl.ds((t % 2) * chan, chan), pl.ds(s * chan, chan)
                    forward[q, t // 2, r, c] = taps[p] if there else none
                    backward[2 - q, t // 2, r, c] = turned[2 - p] if there else none

    def dots(v, blocks, q, lo, hi):
        out = None
        for h in range(2):
            left_side = v[q, h:h + pairs, lo:hi, :].reshape(pairs * (hi - lo), lanes)
            term = jnp.dot(left_side, blocks[q, h], preferred_element_type=F32)
            out = term if out is None else out + term
        return out.reshape(pairs, hi - lo, lanes)

    def conv(v, blocks):
        return dots(v, blocks, 0, 0, cells) + dots(v, blocks, 1, 0, cells) + dots(v, blocks, 2, 0, cells)

    def kernel_grad(kind, v, g):
        upstream = g[...].reshape(rows, lanes)
        for q in range(3):
            low, high = [
                lax.dot_general(v[q, h:h + pairs].reshape(rows, lanes), upstream, (((0,), (0,)), ((), ())), preferred_element_type=F32)
                for h in range(2)
            ]
            taps = (
                low[:chan, :chan] + low[chan:, chan:],
                low[chan:, :chan] + high[:chan, chan:],
                high[:chan, :chan] + high[chan:, chan:],
            )
            for p in range(3):
                at = (p * 3 + q) * chan
                value = taps[p].astype(BF16)
                first = min(max(half - at, 0), chan)
                if first > 0:
                    wsend[kind, 0, at:at + first] = value[:first]
                if first < chan:
                    wsend[kind, 1, at + first - half:at + chan - half] = value[first:]

    def core_copy(kind):
        return to_device(wsend.at[kind, 1 - core], crecv.at[kind], cs_sem.at[kind], cr_sem.at[kind], sibling)

    def reduce_send(kind):
        core_copy(kind).wait_recv()
        both = wsend[kind, core].astype(F32) + crecv[kind].astype(F32)
        rsrc[kind] = both.astype(BF16).reshape(n_own, own_rows, chan)
        for o in range(n_own):
            lon, place = o // per_plane, o % per_plane

            @pl.when(my_own_or_none != o)
            def _():
                to_device(rsrc.at[kind, o], rrecv.at[kind, my_chip], rs_sem.at[kind], rr_sem.at[kind],
                          (lon, place * 2 + core)).start()

        @pl.when(is_own)
        def _():
            rrecv[kind, pl.ds(my_chip, 1)] = rsrc[kind, pl.ds(my_own, 1)]

    my_own_or_none = jnp.where(is_own, my_own, n_own)

    def reduce_wait(kind):
        wait_bytes(rrecv.at[kind, pl.ds(0, chips - 1)], rr_sem.at[kind])
        return jnp.sum(rrecv[kind].astype(F32), axis=0)

    def gather_send(which, value):
        ag[which, core, pl.ds(my_own, 1)] = value.astype(BF16)[None]
        for k in range(1, chips):
            t = (my_chip + k) % chips
            to_device(ag.at[which, core, my_own], ag.at[which, core, my_own], gs_sem.at[which], gr_sem.at[which],
                      (t // plane, (t % plane) * 2 + core)).start()

    def forward_copy(which):
        return to_device(ag.at[which, core], ag.at[which, core], fs_sem.at[which], fr_sem.at[which], sibling)

    def gather_wait(which):
        @pl.when(is_own)
        def _():
            wait_bytes(ag.at[which, core, pl.ds(0, n_own - 1)], gr_sem.at[which])

        @pl.when(jnp.logical_not(is_own))
        def _():
            wait_bytes(ag.at[which, core], gr_sem.at[which])

    def share(index, buf, rows_to_send):
        buf[pl.ds(me, 1)] = jnp.concatenate(rows_to_send, axis=-1)[None]
        for k in range(1, n_dev):
            to_device(buf.at[me], buf.at[me], as_sem.at[index], ar_sem.at[index], device((me + k) % n_dev)).start()

    def shared(index, buf):
        wait_bytes(buf.at[pl.ds(0, n_dev - 1)], ar_sem.at[index])
        return [buf[:, :, i * chan:(i + 1) * chan] for i in range(buf.shape[2] // chan)]

    def fold(field):
        both = jnp.sum(field, axis=(0, 1), keepdims=True)[0]
        return both[:, :chan] + both[:, chan:]

    def over_devices(part):
        return jnp.sum(part, axis=0)

    def moments(act):
        sums = fold(act)
        mean = sums * (1.0 / local)
        dev = act - twice(mean)[None]
        return sums, mean, fold(dev * dev), dev

    def merged(sums, squares):
        mean = over_devices(sums) * (1.0 / total)
        off = sums * (1.0 / local) - mean[None]
        var = (over_devices(squares) + local * over_devices(off * off)) * (1.0 / total)
        return mean, lax.rsqrt(var + 1e-05), off

    def wide(row):
        return twice(row)[None]

    wait_bytes(xin, load_sem.at[0])
    x = xin[...].reshape(pairs, cells, lanes)
    halo_put(H_X, x)
    pl.semaphore_wait(barrier, n_dev - 1)
    halo_send(H_X)
    pack_inner(vx, x)
    for ref in (vx, vn, vp):
        clear_pads(ref)
    wait_bytes(w1f, load_sem.at[2])
    kernel_blocks(kc1, kd1, w1f)

    inner = 2 * samples
    z1[...] = dots(vx, kc1, 1, 0, cells)
    z1[:, inner:, :] += dots(vx, kc1, 0, inner, cells)
    z1[:, :cells - inner, :] += dots(vx, kc1, 2, 0, cells - inner)
    wait_bytes(cot, load_sem.at[1])
    c = cot[...].reshape(pairs, cells, lanes)
    halo_put(H_COT, c)
    halo_send(H_COT)
    share(0, ar0, [fold(c)])
    wait_bytes(par, load_sem.at[4])
    halo_wait(H_X)
    west, east = halo_get(H_X)
    pack_edges(vx, xin, west, east)
    z1[:, :inner, :] += dots(vx, kc1, 0, 0, inner)
    z1[:, cells - inner:, :] += dots(vx, kc1, 2, cells - inner, cells)

    pre = z1[...] + wide(param(B1))
    act, slope = silu_parts(pre)
    a1[...] = act
    slope1[...] = slope
    sums, _, squares, _ = moments(a1[...])
    share(1, ar1, [sums, squares])
    z1[...] = pre
    halo_put(H_Z1, pre)
    halo_send(H_Z1)

    wait_bytes(w2f, load_sem.at[3])
    kernel_blocks(kc2, kd2, w2f)
    gbuf[...] = slope1[...].astype(BF16)
    sum_slope1 = fold(slope1[...])
    kernel_grad(R_B, vx, gbuf)
    core_copy(R_B).start()
    halo_wait(H_Z1)
    z1_halo = halo_get(H_Z1)
    reduce_send(R_B)

    (cot_sums,) = shared(0, ar0)
    shift_two = over_devices(cot_sums)
    cot_mean = shift_two * (1.0 / total)
    mean1, inv1, _ = merged(*shared(1, ar1))
    scale1 = param(G1) * inv1
    shift1 = param(S1) - mean1 * scale1

    def norm_one(a):
        return a * wide(scale1) + wide(shift1)

    pack(vn, norm_one(a1[...]), *[norm_one(silu_parts(z)[0]) for z in z1_halo])
    pre = conv(vn, kc2) + wide(param(B2))
    act, slope = silu_parts(pre)
    a2[...] = act
    slope2[...] = slope
    sums, _, squares, dev = moments(a2[...])
    c = cot[...].reshape(pairs, cells, lanes) - wide(cot_mean)
    share(2, ar2, [sums, squares, fold(c * dev)])
    halo_put(H_Z2, pre)
    halo_send(H_Z2)

    def xhat_one(a):
        return (a - wide(mean1)) * wide(inv1)

    slope_xhat = slope1[...] * xhat_one(a1[...])
    gbuf[...] = slope_xhat.astype(BF16)
    sum_slope_xhat1 = fold(slope_xhat)
    kernel_grad(R_C, vx, gbuf)
    core_copy(R_C).start()
    halo_wait(H_Z2)
    halo_wait(H_COT)
    z2_halo, cot_halo = halo_get(H_Z2), halo_get(H_COT)
    reduce_send(R_C)

    sums2, squares2, cross2 = shared(2, ar2)
    mean2, inv2, off2 = merged(sums2, squares2)
    centred = cot_sums - local * cot_mean[None]
    gain_two = inv2 * (over_devices(cross2) + over_devices(off2 * centred))
    lead2 = param(G2) * inv2

    def pre_two_grad(a, slope, c):
        xhat = (a - wide(mean2)) * wide(inv2)
        return wide(lead2) * (c - wide(cot_mean) - xhat * wide(gain_two * (1.0 / total))) * slope

    grads = []
    for z, ch in zip(z2_halo, cot_halo):
        a, s = silu_parts(z)
        grads.append(pre_two_grad(a, s, ch))
    grad = pre_two_grad(a2[...], slope2[...], cot[...].reshape(pairs, cells, lanes))
    gptg[...] = grad.astype(BF16)
    pack(vp, grad, *grads)
    dref[...] = conv(vp, kd2)

    scaled = dref[...] * slope1[...]
    gbuf[...] = scaled.astype(BF16)
    kernel_grad(R_A, vx, gbuf)
    core_copy(R_A).start()
    d = dref[...]
    share(3, ar3, [fold(d), fold(d * xhat_one(a1[...])), fold(d * slope1[...]), sum_slope1, sum_slope_xhat1,
                   fold(gptg[...].astype(F32))])
    halo_put(H_D, d)
    halo_send(H_D)
    reduce_send(R_A)
    kernel_grad(R_W2, vn, gptg)
    core_copy(R_W2).start()
    xhat2 = (a2[...] - wide(mean2)) * wide(inv2)
    y_ref[...] = (xin[...].reshape(pairs, cells, lanes) + xhat2 * wide(param(G2)) + wide(param(S2))).reshape(y_ref.shape)
    reduce_send(R_W2)

    halo_wait(H_D)
    d_halo = halo_get(H_D)
    shift_one, gain_one, sum_scaled, all_slope, all_slope_xhat, bias_two = [over_devices(part) for part in shared(3, ar3)]
    lead1 = param(G1) * inv1
    shift_mean, gain_mean = shift_one * (1.0 / total), gain_one * (1.0 / total)
    bias_one = lead1 * (sum_scaled - shift_mean * all_slope - gain_mean * all_slope_xhat)
    for i, row in enumerate((bias_one, gain_one, shift_one, bias_two, gain_two, shift_two)):
        vec_ref[i] = row

    def pre_one_grad(a, slope, d):
        return wide(lead1) * (d - wide(shift_mean) - xhat_one(a) * wide(gain_mean)) * slope

    grads = []
    for z, dh in zip(z1_halo, d_halo):
        a, s = silu_parts(z)
        grads.append(pre_one_grad(a, s, dh))
    pack(vp, pre_one_grad(a1[...], slope1[...], dref[...]), *grads)
    ig_ref[...] = (cot[...].reshape(pairs, cells, lanes) + conv(vp, kd1)).reshape(ig_ref.shape)

    @pl.when(is_own)
    def _():
        part_b = reduce_wait(R_B)
        part_c = reduce_wait(R_C)
        part_a = reduce_wait(R_A)
        gather_send(0, lead1 * (part_a - shift_mean * part_b - gain_mean * part_c))
        gather_send(1, reduce_wait(R_W2))

    for which, out in ((0, wg1_ref), (1, wg2_ref)):
        gather_wait(which)
        forward_copy(which).start()
    for which, out in ((0, wg1_ref), (1, wg2_ref)):
        forward_copy(which).wait_recv()
        out[...] = ag[which].astype(F32).reshape(out.shape)

    for kind in range(5):
        for copy in halo_copies(kind):
            copy.wait_send()
    for i, buf in enumerate((ar0, ar1, ar2, ar3)):
        wait_bytes(buf.at[pl.ds(0, n_dev - 1)], as_sem.at[i])
    for kind in range(4):
        core_copy(kind).wait_send()

    @pl.when(is_own)
    def _():
        for kind in range(4):
            wait_bytes(rsrc.at[kind, pl.ds(0, n_own - 1)], rs_sem.at[kind])
        for which in range(2):
            wait_bytes(rrecv.at[which, pl.ds(0, chips - 1)], gs_sem.at[which])

    @pl.when(jnp.logical_not(is_own))
    def _():
        for kind in range(4):
            wait_bytes(rsrc.at[kind], rs_sem.at[kind])

    for which in range(2):
        forward_copy(which).wait_send()


def write_kernel(y, ig, wg1, wg2, vec, y_hbm, ig_hbm, wg1_hbm, wg2_hbm, r0, r1, r2, r3, r4, r5, sem):
    samples, chan = y.shape[2], vec.shape[2]
    copies = []
    for i, (src, dst) in enumerate(((y, y_hbm), (ig, ig_hbm))):
        copies += [
            pltpu.make_async_copy(src.at[:, :, b, pl.ds(s * chan, chan)], dst.at[b, :, s], sem.at[i])
            for b in range(samples)
            for s in range(2)
        ]
    copies += [pltpu.make_async_copy(wg1, wg1_hbm, sem.at[2]), pltpu.make_async_copy(wg2, wg2_hbm, sem.at[3])]
    copies += [pltpu.make_async_copy(vec.at[i], row, sem.at[4 + i]) for i, row in enumerate((r0, r1, r2, r3, r4, r5))]
    for copy in copies:
        copy.start()
    for i, (src, dst) in enumerate(((y, y_hbm), (ig, ig_hbm))):
        pltpu.make_async_copy(src, src, sem.at[i]).wait()
    for copy in copies[-8:]:
        copy.wait()


def on_device(n_lon, n_batch, inputs, weight_one, bias_one, first_norm_scale, first_norm_bias, weight_two, bias_two,
              second_norm_scale, second_norm_bias, cotangent):
    samples, lat, width, chan = inputs.shape
    pairs, cells, lanes = lat // 2, width * samples, 2 * chan
    n_dev = n_lon * n_batch
    chips = n_dev // 2
    half = 9 * chan // 2
    n_own, tiles = owners_of(chips, half // 16)
    own_rows = tiles * 16
    field = (pairs, width, samples, lanes)
    flat = (pairs, cells, lanes)
    split = (samples, pairs, 2, width, chan)
    hbm = pl.BlockSpec(memory_space=pltpu.HBM)
    vmem = pl.BlockSpec(memory_space=VMEM)

    shifted = VMEM((3, pairs + 1, cells, lanes), BF16)
    blocks = VMEM((3, 2, lanes, lanes), BF16)
    scratch = [
        VMEM(field, F32), VMEM(field, F32), VMEM((9 * chan, chan), F32), VMEM((9 * chan, chan), F32), VMEM((6, 1, chan), F32),
        shifted, shifted, shifted, blocks, blocks, blocks, blocks,
        VMEM(flat, F32), VMEM(flat, F32), VMEM(flat, F32), VMEM(flat, F32), VMEM(flat, F32), VMEM(flat, F32),
        VMEM(flat, BF16), VMEM(flat, BF16),
        VMEM((5, 2, pairs * samples, lanes), BF16), VMEM((5, 2, pairs * samples, lanes), BF16),
        VMEM((n_dev, 1, chan), F32), VMEM((n_dev, 1, 2 * chan), F32), VMEM((n_dev, 1, 3 * chan), F32), VMEM((n_dev, 1, 6 * chan), F32),
        VMEM((4, 2, half, chan), BF16), VMEM((4, half, chan), BF16), VMEM((4, n_own, own_rows, chan), BF16),
        VMEM((4, chips, own_rows, chan), BF16), VMEM((2, 2, n_own, own_rows, chan), BF16),
        DMA((5,)), DMA((5, 2)), DMA((5, 2)), DMA((4,)), DMA((4,)), DMA((4,)), DMA((4,)), DMA((4,)), DMA((4,)),
        DMA((2,)), DMA((2,)), DMA((2,)), DMA((2,)),
    ]
    small = (bias_one, first_norm_scale, first_norm_bias, bias_two, second_norm_scale, second_norm_bias)
    y, ig, wg1, wg2, vec = pl.pallas_call(
        functools.partial(main_kernel, n_lon, n_batch),
        out_shape=(VMEM(field, F32), VMEM(field, F32), VMEM((9 * chan, chan), F32), VMEM((9 * chan, chan), F32), VMEM((6, 1, chan), F32)),
        in_specs=[hbm] * 10,
        out_specs=(vmem,) * 5,
        scratch_shapes=scratch,
        compiler_params=pltpu.CompilerParams(collective_id=0, has_side_effects=True, vmem_limit_bytes=44 * 2**20),
        name="block",
    )(inputs.reshape(split), cotangent.reshape(split), weight_one.reshape(9 * chan, chan), weight_two.reshape(9 * chan, chan),
      *[v.reshape(1, chan) for v in small])
    outs = pl.pallas_call(
        write_kernel,
        out_shape=(jax.ShapeDtypeStruct(split, F32),) * 2 + (jax.ShapeDtypeStruct((9 * chan, chan), F32),) * 2
        + (jax.ShapeDtypeStruct((1, chan), F32),) * 6,
        in_specs=[vmem] * 5,
        out_specs=(hbm,) * 10,
        scratch_shapes=[DMA((10,))],
        name="write",
    )(y, ig, wg1, wg2, vec)
    rows = [v.reshape(chan) for v in outs[4:]]
    return (outs[0].reshape(inputs.shape), outs[1].reshape(inputs.shape), outs[2].reshape(3, 3, chan, chan), rows[0], rows[1], rows[2],
            outs[3].reshape(3, 3, chan, chan), rows[3], rows[4], rows[5])


def solution(mesh):
    wide = P("batch", None, "lon", None)
    return jax.shard_map(
        functools.partial(on_device, mesh.shape["lon"], mesh.shape["batch"]),
        mesh=mesh,
        in_specs=(wide,) + (P(),) * 8 + (wide,),
        out_specs=(wide, wide) + (P(),) * 8,
        check_vma=False,
    )
```

```python
import functools

import jax
import jax.numpy as jnp
from jax import lax
from jax.experimental import pallas as pl
from jax.experimental.pallas import tpu as pltpu
from jax.sharding import PartitionSpec as P

MESH = pl.DeviceIdType.MESH
F32, BF16 = jnp.float32, jnp.bfloat16
VMEM = pltpu.VMEM
DMA = pltpu.SemaphoreType.DMA

H_X, H_COT, H_Z1, H_Z2, H_D = range(5)
R_A, R_B, R_C, R_W2 = range(4)
B1, G1, S1, B2, G2, S2 = range(6)


def twice(row):
    return jnp.concatenate([row, row], axis=-1)


def silu_parts(pre):
    sig = 0.5 * jnp.tanh(0.5 * pre) + 0.5
    return pre * sig, sig * (1.0 + pre * (1.0 - sig))


def owners_of(chips, tiles):
    for size in range(1, tiles + 1):
        if tiles % size == 0 and tiles // size <= chips:
            return tiles // size, size


def main_kernel(n_lon, n_batch, x_hbm, cot_hbm, w1_hbm, w2_hbm, b1_hbm, g1_hbm, s1_hbm, b2_hbm, g2_hbm, s2_hbm,
                y_ref, ig_ref, wg1_ref, wg2_ref, vec_ref,
                xin, cot, w1f, w2f, par, vx, vn, vp, kc1, kc2, kd1, kd2, z1, a1, slope1, a2, slope2, dref, gbuf, gptg,
                hsend, hrecv, ar0, ar1, ar2, ar3, wsend, crecv, rsrc, rrecv, ag,
                load_sem, hs_sem, hr_sem, as_sem, ar_sem, cs_sem, cr_sem, rs_sem, rr_sem, gs_sem, gr_sem, fs_sem, fr_sem):
    samples, pairs, _, width, chan = x_hbm.shape
    lanes, cells = 2 * chan, width * samples
    rows = pairs * cells
    n_dev = n_lon * n_batch
    chips, plane = n_dev // 2, n_batch // 2
    local = 2.0 * rows
    total = local * n_dev
    n_own, own_rows = rsrc.shape[1], rsrc.shape[2]
    per_plane = -(-n_own // n_lon)
    half = wsend.shape[2]

    my_lon, my_batch = lax.axis_index("lon"), lax.axis_index("batch")
    me = my_lon * n_batch + my_batch
    core, my_place = my_batch % 2, my_batch // 2
    my_chip = my_lon * plane + my_place
    my_own = my_lon * per_plane + my_place
    is_own = jnp.logical_and(my_place < per_plane, my_own < n_own)
    sibling = (my_lon, my_batch + 1 - 2 * core)
    left = ((my_lon + n_lon - 1) % n_lon, my_batch)
    right = ((my_lon + 1) % n_lon, my_batch)

    def device(t):
        return (t // n_batch, t % n_batch)

    def to_device(src, dst, send, recv, where):
        return pltpu.make_async_remote_copy(src, dst, send, recv, device_id=where, device_id_type=MESH)

    def wait_bytes(ref, sem):
        pltpu.make_async_copy(ref, ref, sem).wait()

    def field_loads(src, dst, sem):
        return [
            pltpu.make_async_copy(src.at[b, :, s], dst.at[:, :, b, pl.ds(s * chan, chan)], sem)
            for b in range(samples)
            for s in range(2)
        ]

    for copy in field_loads(x_hbm, xin, load_sem.at[0]):
        copy.start()
    pltpu.make_async_copy(w1_hbm, w1f, load_sem.at[2]).start()
    for copy in field_loads(cot_hbm, cot, load_sem.at[1]):
        copy.start()
    pltpu.make_async_copy(w2_hbm, w2f, load_sem.at[3]).start()
    for i, src in enumerate((b1_hbm, g1_hbm, s1_hbm, b2_hbm, g2_hbm, s2_hbm)):
        pltpu.make_async_copy(src, par.at[i], load_sem.at[4]).start()

    barrier = pltpu.get_barrier_semaphore()
    for k in range(1, n_dev):
        pl.semaphore_signal(barrier, inc=1, device_id=device((me + k) % n_dev), device_id_type=MESH)

    def param(i):
        return par[i]

    def column(field, j):
        return field[:, j * samples:(j + 1) * samples, :]

    def halo_copies(kind):
        return (
            to_device(hsend.at[kind, 0], hrecv.at[kind, 1], hs_sem.at[kind, 0], hr_sem.at[kind, 1], left),
            to_device(hsend.at[kind, 1], hrecv.at[kind, 0], hs_sem.at[kind, 1], hr_sem.at[kind, 0], right),
        )

    def halo_put(kind, field):
        hsend[kind, 0] = column(field, 0).reshape(pairs * samples, lanes).astype(BF16)
        hsend[kind, 1] = column(field, width - 1).reshape(pairs * samples, lanes).astype(BF16)

    def halo_send(kind):
        for copy in halo_copies(kind):
            copy.start()

    def halo_wait(kind):
        for copy in halo_copies(kind):
            copy.wait_recv()

    def halo_get(kind):
        return [hrecv[kind, side].astype(F32).reshape(pairs, samples, lanes) for side in range(2)]

    def pack(ref, field, west, east):
        for s in range(2):
            part = field[:, :, s * chan:(s + 1) * chan]
            at = (slice(s, s + pairs), slice(None), slice((1 - s) * chan, (2 - s) * chan))
            ref[(1,) + at] = part.astype(BF16)
            lo = west[:, :, s * chan:(s + 1) * chan]
            hi = east[:, :, s * chan:(s + 1) * chan]
            ref[(0,) + at] = jnp.concatenate([lo, part[:, :-samples]], axis=1).astype(BF16)
            ref[(2,) + at] = jnp.concatenate([part[:, samples:], hi], axis=1).astype(BF16)

    def pack_inner(ref, field):
        for s in range(2):
            part = field[:, :, s * chan:(s + 1) * chan]
            rows_at, lanes_at = slice(s, s + pairs), slice((1 - s) * chan, (2 - s) * chan)
            ref[1, rows_at, :, lanes_at] = part.astype(BF16)
            ref[0, rows_at, 2 * samples:, lanes_at] = part[:, samples:-samples].astype(BF16)
            ref[2, rows_at, :cells - 2 * samples, lanes_at] = part[:, samples:-samples].astype(BF16)

    def pack_edges(ref, field_ref, west, east):
        first = field_ref[:, 0]
        last = field_ref[:, width - 1]
        for s in range(2):
            rows_at, lanes_at = slice(s, s + pairs), slice((1 - s) * chan, (2 - s) * chan)
            cut = slice(s * chan, (s + 1) * chan)
            ref[0, rows_at, :2 * samples, lanes_at] = jnp.concatenate([west[:, :, cut], first[:, :, cut]], axis=1).astype(BF16)
            ref[2, rows_at, cells - 2 * samples:, lanes_at] = jnp.concatenate([last[:, :, cut], east[:, :, cut]], axis=1).astype(BF16)

    def clear_pads(ref):
        for q in range(3):
            ref[q, 0, :, :chan] = jnp.zeros((cells, chan), BF16)
            ref[q, pairs, :, chan:] = jnp.zeros((cells, chan), BF16)

    def kernel_blocks(forward, backward, weight):
        none = jnp.zeros((chan, chan), BF16)
        for q in range(3):
            taps = [weight[pl.ds((p * 3 + q) * chan, chan), :].astype(BF16) for p in range(3)]
            turned = [tap.T for tap in taps]
            for t in range(4):
                for s in range(2):
                    p = t - s
                    there = 0 <= p <= 2
                    r, c = pl.ds((t % 2) * chan, chan), pl.ds(s * chan, chan)
                    forward[q, t // 2, r, c] = taps[p] if there else none
                    backward[2 - q, t // 2, r, c] = turned[2 - p] if there else none

    def dots(v, blocks, q, lo, hi):
        out = None
        for h in range(2):
            left_side = v[q, h:h + pairs, lo:hi, :].reshape(pairs * (hi - lo), lanes)
            term = jnp.dot(left_side, blocks[q, h], preferred_element_type=F32)
            out = term if out is None else out + term
        return out.reshape(pairs, hi - lo, lanes)

    def conv(v, blocks):
        return dots(v, blocks, 0, 0, cells) + dots(v, blocks, 1, 0, cells) + dots(v, blocks, 2, 0, cells)

    def kernel_grad(kind, v, g):
        upstream = g[...].reshape(rows, lanes)
        for q in range(3):
            low, high = [
                lax.dot_general(v[q, h:h + pairs].reshape(rows, lanes), upstream, (((0,), (0,)), ((), ())), preferred_element_type=F32)
                for h in range(2)
            ]
            taps = (
                low[:chan, :chan] + low[chan:, chan:],
                low[chan:, :chan] + high[:chan, chan:],
                high[:chan, :chan] + high[chan:, chan:],
            )
            for p in range(3):
                at = (p * 3 + q) * chan
                value = taps[p].astype(BF16)
                first = min(max(half - at, 0), chan)
                if first > 0:
                    wsend[kind, 0, at:at + first] = value[:first]
                if first < chan:
                    wsend[kind, 1, at + first - half:at + chan - half] = value[first:]

    def core_copy(kind):
        return to_device(wsend.at[kind, 1 - core], crecv.at[kind], cs_sem.at[kind], cr_sem.at[kind], sibling)

    def reduce_send(kind):
        core_copy(kind).wait_recv()
        both = wsend[kind, core].astype(F32) + crecv[kind].astype(F32)
        rsrc[kind] = both.astype(BF16).reshape(n_own, own_rows, chan)
        for o in range(n_own):
            lon, place = o // per_plane, o % per_plane

            @pl.when(my_own_or_none != o)
            def _():
                to_device(rsrc.at[kind, o], rrecv.at[kind, my_chip], rs_sem.at[kind], rr_sem.at[kind],
                          (lon, place * 2 + core)).start()

        @pl.when(is_own)
        def _():
            rrecv[kind, pl.ds(my_chip, 1)] = rsrc[kind, pl.ds(my_own, 1)]

    my_own_or_none = jnp.where(is_own, my_own, n_own)

    def reduce_wait(kind):
        wait_bytes(rrecv.at[kind, pl.ds(0, chips - 1)], rr_sem.at[kind])
        return jnp.sum(rrecv[kind].astype(F32), axis=0)

    def gather_send(which, value):
        ag[which, core, pl.ds(my_own, 1)] = value.astype(BF16)[None]
        for k in range(1, chips):
            t = (my_chip + k) % chips
            to_device(ag.at[which, core, my_own], ag.at[which, core, my_own], gs_sem.at[which], gr_sem.at[which],
                      (t // plane, (t % plane) * 2 + core)).start()

    def forward_copy(which):
        return to_device(ag.at[which, core], ag.at[which, core], fs_sem.at[which], fr_sem.at[which], sibling)

    def gather_wait(which):
        @pl.when(is_own)
        def _():
            wait_bytes(ag.at[which, core, pl.ds(0, n_own - 1)], gr_sem.at[which])

        @pl.when(jnp.logical_not(is_own))
        def _():
            wait_bytes(ag.at[which, core], gr_sem.at[which])

    def share(index, buf, rows_to_send):
        buf[pl.ds(me, 1)] = jnp.concatenate(rows_to_send, axis=-1)[None]
        for k in range(1, n_dev):
            to_device(buf.at[me], buf.at[me], as_sem.at[index], ar_sem.at[index], device((me + k) % n_dev)).start()

    def shared(index, buf):
        wait_bytes(buf.at[pl.ds(0, n_dev - 1)], ar_sem.at[index])
        return [buf[:, :, i * chan:(i + 1) * chan] for i in range(buf.shape[2] // chan)]

    def fold(field):
        both = jnp.sum(field, axis=(0, 1), keepdims=True)[0]
        return both[:, :chan] + both[:, chan:]

    def over_devices(part):
        return jnp.sum(part, axis=0)

    def moments(act):
        sums = fold(act)
        mean = sums * (1.0 / local)
        dev = act - twice(mean)[None]
        return sums, mean, fold(dev * dev), dev

    def merged(sums, squares):
        mean = over_devices(sums) * (1.0 / total)
        off = sums * (1.0 / local) - mean[None]
        var = (over_devices(squares) + local * over_devices(off * off)) * (1.0 / total)
        return mean, lax.rsqrt(var + 1e-05), off

    def wide(row):
        return twice(row)[None]

    wait_bytes(xin, load_sem.at[0])
    x = xin[...].reshape(pairs, cells, lanes)
    halo_put(H_X, x)
    pl.semaphore_wait(barrier, n_dev - 1)
    halo_send(H_X)
    pack_inner(vx, x)
    for ref in (vx, vn, vp):
        clear_pads(ref)
    wait_bytes(w1f, load_sem.at[2])
    kernel_blocks(kc1, kd1, w1f)

    inner = 2 * samples
    z1[...] = dots(vx, kc1, 1, 0, cells)
    z1[:, inner:, :] += dots(vx, kc1, 0, inner, cells)
    z1[:, :cells - inner, :] += dots(vx, kc1, 2, 0, cells - inner)
    wait_bytes(cot, load_sem.at[1])
    c = cot[...].reshape(pairs, cells, lanes)
    halo_put(H_COT, c)
    halo_send(H_COT)
    share(0, ar0, [fold(c)])
    wait_bytes(par, load_sem.at[4])
    halo_wait(H_X)
    west, east = halo_get(H_X)
    pack_edges(vx, xin, west, east)
    z1[:, :inner, :] += dots(vx, kc1, 0, 0, inner)
    z1[:, cells - inner:, :] += dots(vx, kc1, 2, cells - inner, cells)

    pre = z1[...] + wide(param(B1))
    act, slope = silu_parts(pre)
    a1[...] = act
    slope1[...] = slope
    sums, _, squares, _ = moments(a1[...])
    share(1, ar1, [sums, squares])
    z1[...] = pre
    halo_put(H_Z1, pre)
    halo_send(H_Z1)

    wait_bytes(w2f, load_sem.at[3])
    kernel_blocks(kc2, kd2, w2f)
    gbuf[...] = slope1[...].astype(BF16)
    sum_slope1 = fold(slope1[...])
    kernel_grad(R_B, vx, gbuf)
    core_copy(R_B).start()
    halo_wait(H_Z1)
    z1_halo = halo_get(H_Z1)
    reduce_send(R_B)

    (cot_sums,) = shared(0, ar0)
    shift_two = over_devices(cot_sums)
    cot_mean = shift_two * (1.0 / total)
    mean1, inv1, _ = merged(*shared(1, ar1))
    scale1 = param(G1) * inv1
    shift1 = param(S1) - mean1 * scale1

    def norm_one(a):
        return a * wide(scale1) + wide(shift1)

    pack(vn, norm_one(a1[...]), *[norm_one(silu_parts(z)[0]) for z in z1_halo])
    pre = conv(vn, kc2) + wide(param(B2))
    act, slope = silu_parts(pre)
    a2[...] = act
    slope2[...] = slope
    sums, _, squares, dev = moments(a2[...])
    c = cot[...].reshape(pairs, cells, lanes) - wide(cot_mean)
    share(2, ar2, [sums, squares, fold(c * dev)])
    halo_put(H_Z2, pre)
    halo_send(H_Z2)

    def xhat_one(a):
        return (a - wide(mean1)) * wide(inv1)

    slope_xhat = slope1[...] * xhat_one(a1[...])
    gbuf[...] = slope_xhat.astype(BF16)
    sum_slope_xhat1 = fold(slope_xhat)
    kernel_grad(R_C, vx, gbuf)
    core_copy(R_C).start()
    halo_wait(H_Z2)
    halo_wait(H_COT)
    z2_halo, cot_halo = halo_get(H_Z2), halo_get(H_COT)
    reduce_send(R_C)

    sums2, squares2, cross2 = shared(2, ar2)
    mean2, inv2, off2 = merged(sums2, squares2)
    centred = cot_sums - local * cot_mean[None]
    gain_two = inv2 * (over_devices(cross2) + over_devices(off2 * centred))
    lead2 = param(G2) * inv2

    def pre_two_grad(a, slope, c):
        xhat = (a - wide(mean2)) * wide(inv2)
        return wide(lead2) * (c - wide(cot_mean) - xhat * wide(gain_two * (1.0 / total))) * slope

    grads = []
    for z, ch in zip(z2_halo, cot_halo):
        a, s = silu_parts(z)
        grads.append(pre_two_grad(a, s, ch))
    grad = pre_two_grad(a2[...], slope2[...], cot[...].reshape(pairs, cells, lanes))
    gptg[...] = grad.astype(BF16)
    pack(vp, grad, *grads)
    dref[...] = conv(vp, kd2)

    scaled = dref[...] * slope1[...]
    gbuf[...] = scaled.astype(BF16)
    kernel_grad(R_A, vx, gbuf)
    core_copy(R_A).start()
    d = dref[...]
    share(3, ar3, [fold(d), fold(d * xhat_one(a1[...])), fold(d * slope1[...]), sum_slope1, sum_slope_xhat1,
                   fold(gptg[...].astype(F32))])
    halo_put(H_D, d)
    halo_send(H_D)
    reduce_send(R_A)
    kernel_grad(R_W2, vn, gptg)
    core_copy(R_W2).start()
    xhat2 = (a2[...] - wide(mean2)) * wide(inv2)
    y_ref[...] = (xin[...].reshape(pairs, cells, lanes) + xhat2 * wide(param(G2)) + wide(param(S2))).reshape(y_ref.shape)
    reduce_send(R_W2)

    halo_wait(H_D)
    d_halo = halo_get(H_D)
    shift_one, gain_one, sum_scaled, all_slope, all_slope_xhat, bias_two = [over_devices(part) for part in shared(3, ar3)]
    lead1 = param(G1) * inv1
    shift_mean, gain_mean = shift_one * (1.0 / total), gain_one * (1.0 / total)
    bias_one = lead1 * (sum_scaled - shift_mean * all_slope - gain_mean * all_slope_xhat)
    for i, row in enumerate((bias_one, gain_one, shift_one, bias_two, gain_two, shift_two)):
        vec_ref[i] = row

    def pre_one_grad(a, slope, d):
        return wide(lead1) * (d - wide(shift_mean) - xhat_one(a) * wide(gain_mean)) * slope

    grads = []
    for z, dh in zip(z1_halo, d_halo):
        a, s = silu_parts(z)
        grads.append(pre_one_grad(a, s, dh))
    pack(vp, pre_one_grad(a1[...], slope1[...], dref[...]), *grads)
    ig_ref[...] = (cot[...].reshape(pairs, cells, lanes) + conv(vp, kd1)).reshape(ig_ref.shape)

    @pl.when(is_own)
    def _():
        part_b = reduce_wait(R_B)
        part_c = reduce_wait(R_C)
        part_a = reduce_wait(R_A)
        gather_send(0, lead1 * (part_a - shift_mean * part_b - gain_mean * part_c))
        gather_send(1, reduce_wait(R_W2))

    for which, out in ((0, wg1_ref), (1, wg2_ref)):
        gather_wait(which)
        forward_copy(which).start()
    for which, out in ((0, wg1_ref), (1, wg2_ref)):
        forward_copy(which).wait_recv()
        out[...] = ag[which].astype(F32).reshape(out.shape)

    for kind in range(5):
        for copy in halo_copies(kind):
            copy.wait_send()
    for i, buf in enumerate((ar0, ar1, ar2, ar3)):
        wait_bytes(buf.at[pl.ds(0, n_dev - 1)], as_sem.at[i])
    for kind in range(4):
        core_copy(kind).wait_send()

    @pl.when(is_own)
    def _():
        for kind in range(4):
            wait_bytes(rsrc.at[kind, pl.ds(0, n_own - 1)], rs_sem.at[kind])
        for which in range(2):
            wait_bytes(rrecv.at[which, pl.ds(0, chips - 1)], gs_sem.at[which])

    @pl.when(jnp.logical_not(is_own))
    def _():
        for kind in range(4):
            wait_bytes(rsrc.at[kind], rs_sem.at[kind])

    for which in range(2):
        forward_copy(which).wait_send()


def write_kernel(y, ig, wg1, wg2, vec, y_hbm, ig_hbm, wg1_hbm, wg2_hbm, r0, r1, r2, r3, r4, r5, sem):
    samples, chan = y.shape[2], vec.shape[2]
    copies = []
    for i, (src, dst) in enumerate(((y, y_hbm), (ig, ig_hbm))):
        copies += [
            pltpu.make_async_copy(src.at[:, :, b, pl.ds(s * chan, chan)], dst.at[b, :, s], sem.at[i])
            for b in range(samples)
            for s in range(2)
        ]
    copies += [pltpu.make_async_copy(wg1, wg1_hbm, sem.at[2]), pltpu.make_async_copy(wg2, wg2_hbm, sem.at[3])]
    copies += [pltpu.make_async_copy(vec.at[i], row, sem.at[4 + i]) for i, row in enumerate((r0, r1, r2, r3, r4, r5))]
    for copy in copies:
        copy.start()
    for i, (src, dst) in enumerate(((y, y_hbm), (ig, ig_hbm))):
        pltpu.make_async_copy(src, src, sem.at[i]).wait()
    for copy in copies[-8:]:
        copy.wait()


def on_device(n_lon, n_batch, inputs, weight_one, bias_one, first_norm_scale, first_norm_bias, weight_two, bias_two,
              second_norm_scale, second_norm_bias, cotangent):
    samples, lat, width, chan = inputs.shape
    pairs, cells, lanes = lat // 2, width * samples, 2 * chan
    n_dev = n_lon * n_batch
    chips = n_dev // 2
    half = 9 * chan // 2
    n_own, tiles = owners_of(chips, half // 16)
    own_rows = tiles * 16
    field = (pairs, width, samples, lanes)
    flat = (pairs, cells, lanes)
    split = (samples, pairs, 2, width, chan)
    hbm = pl.BlockSpec(memory_space=pltpu.HBM)
    vmem = pl.BlockSpec(memory_space=VMEM)

    shifted = VMEM((3, pairs + 1, cells, lanes), BF16)
    blocks = VMEM((3, 2, lanes, lanes), BF16)
    scratch = [
        VMEM(field, F32), VMEM(field, F32), VMEM((9 * chan, chan), F32), VMEM((9 * chan, chan), F32), VMEM((6, 1, chan), F32),
        shifted, shifted, shifted, blocks, blocks, blocks, blocks,
        VMEM(flat, F32), VMEM(flat, F32), VMEM(flat, F32), VMEM(flat, F32), VMEM(flat, F32), VMEM(flat, F32),
        VMEM(flat, BF16), VMEM(flat, BF16),
        VMEM((5, 2, pairs * samples, lanes), BF16), VMEM((5, 2, pairs * samples, lanes), BF16),
        VMEM((n_dev, 1, chan), F32), VMEM((n_dev, 1, 2 * chan), F32), VMEM((n_dev, 1, 3 * chan), F32), VMEM((n_dev, 1, 6 * chan), F32),
        VMEM((4, 2, half, chan), BF16), VMEM((4, half, chan), BF16), VMEM((4, n_own, own_rows, chan), BF16),
        VMEM((4, chips, own_rows, chan), BF16), VMEM((2, 2, n_own, own_rows, chan), BF16),
        DMA((5,)), DMA((5, 2)), DMA((5, 2)), DMA((4,)), DMA((4,)), DMA((4,)), DMA((4,)), DMA((4,)), DMA((4,)),
        DMA((2,)), DMA((2,)), DMA((2,)), DMA((2,)),
    ]
    small = (bias_one, first_norm_scale, first_norm_bias, bias_two, second_norm_scale, second_norm_bias)
    y, ig, wg1, wg2, vec = pl.pallas_call(
        functools.partial(main_kernel, n_lon, n_batch),
        out_shape=(VMEM(field, F32), VMEM(field, F32), VMEM((9 * chan, chan), F32), VMEM((9 * chan, chan), F32), VMEM((6, 1, chan), F32)),
        in_specs=[hbm] * 10,
        out_specs=(vmem,) * 5,
        scratch_shapes=scratch,
        compiler_params=pltpu.CompilerParams(collective_id=0, has_side_effects=True, vmem_limit_bytes=44 * 2**20),
        name="block",
    )(*[
        pltpu.with_memory_space_constraint(v, pltpu.HBM)
        for v in (inputs.reshape(split), cotangent.reshape(split), weight_one.reshape(9 * chan, chan),
                  weight_two.reshape(9 * chan, chan), *[v.reshape(1, chan) for v in small])
    ])
    outs = pl.pallas_call(
        write_kernel,
        out_shape=(jax.ShapeDtypeStruct(split, F32),) * 2 + (jax.ShapeDtypeStruct((9 * chan, chan), F32),) * 2
        + (jax.ShapeDtypeStruct((1, chan), F32),) * 6,
        in_specs=[vmem] * 5,
        out_specs=(hbm,) * 10,
        scratch_shapes=[DMA((10,))],
        name="write",
    )(*[pltpu.with_memory_space_constraint(v, VMEM) for v in (y, ig, wg1, wg2, vec)])
    rows = [v.reshape(chan) for v in outs[4:]]
    return (outs[0].reshape(inputs.shape), outs[1].reshape(inputs.shape), outs[2].reshape(3, 3, chan, chan), rows[0], rows[1], rows[2],
            outs[3].reshape(3, 3, chan, chan), rows[3], rows[4], rows[5])


def solution(mesh):
    wide = P("batch", None, "lon", None)
    return jax.shard_map(
        functools.partial(on_device, mesh.shape["lon"], mesh.shape["batch"]),
        mesh=mesh,
        in_specs=(wide,) + (P(),) * 8 + (wide,),
        out_specs=(wide, wide) + (P(),) * 8,
        check_vma=False,
    )
```

```python
import functools

import jax
import jax.numpy as jnp
from jax import lax
from jax.experimental import pallas as pl
from jax.experimental.pallas import tpu as pltpu
from jax.sharding import PartitionSpec as P

MESH = pl.DeviceIdType.MESH
F32, BF16 = jnp.float32, jnp.bfloat16
VMEM = pltpu.VMEM
DMA = pltpu.SemaphoreType.DMA

H_X, H_COT, H_Z1, H_Z2, H_D = range(5)
R_B, R_C, R_W2, R_A = range(4)
B1, G1, S1, B2, G2, S2 = range(6)


def twice(row):
    return jnp.concatenate([row, row], axis=-1)


def silu_parts(pre):
    sig = 0.5 * jnp.tanh(0.5 * pre) + 0.5
    return pre * sig, sig * (1.0 + pre * (1.0 - sig))


def places_of(plane, tiles):
    return max(d for d in range(1, min(plane, tiles) + 1) if tiles % d == 0)


def main_kernel(n_lon, n_batch, x_hbm, cot_hbm, w1_hbm, w2_hbm, b1_hbm, g1_hbm, s1_hbm, b2_hbm, g2_hbm, s2_hbm,
                y_ref, ig_ref, wg1_ref, wg2_ref, vec_ref,
                xin, cot, w1f, w2f, par, vx, vn, vp, kc1, kc2, kd1, kd2, z1, a1, slope1, z2, a2, slope2, dref, gbuf, gpair, parts,
                hsend, hrecv, ar1, ar2, ar3, ar4, wsend, crecv, rsrc, prec, zrec, ag, sems):
    samples, pairs, _, width, chan = x_hbm.shape
    lanes, cells = 2 * chan, width * samples
    rows = pairs * cells
    n_dev = n_lon * n_batch
    plane = n_batch // 2
    local = 2.0 * rows
    total = local * n_dev
    half = wsend.shape[3]
    n_place, part_rows = rsrc.shape[2], rsrc.shape[3]

    my_lon, my_batch = lax.axis_index("lon"), lax.axis_index("batch")
    me = my_lon * n_batch + my_batch
    core, my_place = my_batch % 2, my_batch // 2
    is_place = my_place < n_place
    sibling = (my_lon, my_batch + 1 - 2 * core)
    left = ((my_lon + n_lon - 1) % n_lon, my_batch)
    right = ((my_lon + 1) % n_lon, my_batch)

    low = my_lon < n_lon // 2
    bands = []
    for j in range(n_lon - 1):
        down, up = n_lon - 1 - j, j
        bands.append(jnp.where(low, jnp.where(down <= my_lon, down - 1, down), jnp.where(up >= my_lon, up + 1, up)))
    others = [(band, (my_batch + k) % n_batch) for band in bands for k in range(n_batch)]
    others += [(my_lon, (my_batch + k) % n_batch) for k in range(1, n_batch)]

    taken = []

    def new_sem():
        taken.append(0)
        return sems.at[len(taken) - 1]

    def to_device(src, dst, send, recv, where):
        return pltpu.make_async_remote_copy(src, dst, send, recv, device_id=where, device_id_type=MESH)

    def wait_bytes(ref, sem):
        pltpu.make_async_copy(ref, ref, sem).wait()

    flying = {}

    def settle(*key):
        flying.pop(key)()

    inner = 2 * samples

    def field_loads(src, dst, sem):
        return [
            pltpu.make_async_copy(src.at[b, :, s], dst.at[:, :, b, pl.ds(s * chan, chan)], sem)
            for b in range(samples)
            for s in range(2)
        ]

    def load(name, copies, ref, sem):
        for copy in copies:
            copy.start()
        flying["load", name] = functools.partial(wait_bytes, ref, sem)

    sem_x, sem_w1, sem_cot, sem_w2, sem_par = [new_sem() for _ in range(5)]
    load("x", field_loads(x_hbm, xin, sem_x), xin, sem_x)
    load("w1", [pltpu.make_async_copy(w1_hbm, w1f, sem_w1)], w1f, sem_w1)
    load("cot", field_loads(cot_hbm, cot, sem_cot), cot, sem_cot)
    load("w2", [pltpu.make_async_copy(w2_hbm, w2f, sem_w2)], w2f, sem_w2)
    smalls = (b1_hbm, g1_hbm, s1_hbm, b2_hbm, g2_hbm, s2_hbm)
    load("par", [pltpu.make_async_copy(src, par.at[i], sem_par) for i, src in enumerate(smalls)], par, sem_par)

    barrier = pltpu.get_barrier_semaphore()
    for where in others:
        pl.semaphore_signal(barrier, inc=1, device_id=where, device_id_type=MESH)

    def param(i):
        return par[i]

    def column(field, j):
        return field[:, j * samples:(j + 1) * samples, :]

    def halo_send(kind, first, last):
        hsend[kind, 0] = first.reshape(pairs * samples, lanes).astype(BF16)
        hsend[kind, 1] = last.reshape(pairs * samples, lanes).astype(BF16)
        to_west = to_device(hsend.at[kind, 0], hrecv.at[kind, 1], new_sem(), new_sem(), left)
        to_east = to_device(hsend.at[kind, 1], hrecv.at[kind, 0], new_sem(), new_sem(), right)
        for copy in (to_west, to_east):
            copy.start()
        flying["halo out", kind] = lambda: (to_west.wait_send(), to_east.wait_send())
        flying["halo", kind] = lambda: (to_west.wait_recv(), to_east.wait_recv())

    def halo_get(kind):
        settle("halo", kind)
        return [hrecv[kind, side].astype(F32).reshape(pairs, samples, lanes) for side in range(2)]

    def pack_inner(ref, field):
        for s in range(2):
            part = field[:, :, s * chan:(s + 1) * chan]
            rows_at, lanes_at = slice(s, s + pairs), slice((1 - s) * chan, (2 - s) * chan)
            ref[1, rows_at, :, lanes_at] = part.astype(BF16)
            ref[0, rows_at, inner:, lanes_at] = part[:, samples:-samples].astype(BF16)
            ref[2, rows_at, :cells - inner, lanes_at] = part[:, samples:-samples].astype(BF16)

    def pack_edges(ref, first, last, west, east):
        for s in range(2):
            rows_at, lanes_at = slice(s, s + pairs), slice((1 - s) * chan, (2 - s) * chan)
            cut = slice(s * chan, (s + 1) * chan)
            ref[0, rows_at, :inner, lanes_at] = jnp.concatenate([west[:, :, cut], first[:, :, cut]], axis=1).astype(BF16)
            ref[2, rows_at, cells - inner:, lanes_at] = jnp.concatenate([last[:, :, cut], east[:, :, cut]], axis=1).astype(BF16)

    def clear_pads(ref):
        for q in range(3):
            ref[q, 0, :, :chan] = jnp.zeros((cells, chan), BF16)
            ref[q, pairs, :, chan:] = jnp.zeros((cells, chan), BF16)

    def kernel_blocks(forward, backward, weight):
        none = jnp.zeros((chan, chan), BF16)
        for q in range(3):
            taps = [weight[pl.ds((p * 3 + q) * chan, chan), :].astype(BF16) for p in range(3)]
            turned = [tap.T for tap in taps]
            for t in range(4):
                for s in range(2):
                    p = t - s
                    there = 0 <= p <= 2
                    r, c = pl.ds((t % 2) * chan, chan), pl.ds(s * chan, chan)
                    forward[q, t // 2, r, c] = taps[p] if there else none
                    backward[2 - q, t // 2, r, c] = turned[2 - p] if there else none

    def dots(v, blocks, q, lo, hi):
        out = None
        for h in range(2):
            left_side = v[q, h:h + pairs, lo:hi, :].reshape(pairs * (hi - lo), lanes)
            term = jnp.dot(left_side, blocks[q, h], preferred_element_type=F32)
            out = term if out is None else out + term
        return out.reshape(pairs, hi - lo, lanes)

    def conv_inner(out, v, blocks):
        out[...] = dots(v, blocks, 1, 0, cells)
        out[:, inner:, :] += dots(v, blocks, 0, inner, cells)
        out[:, :cells - inner, :] += dots(v, blocks, 2, 0, cells - inner)

    def conv_edges(out, v, blocks):
        out[:, :inner, :] += dots(v, blocks, 0, 0, inner)
        out[:, cells - inner:, :] += dots(v, blocks, 2, cells - inner, cells)

    def first_last(ref):
        return ref[:, :samples, :], ref[:, cells - samples:, :]

    def kernel_grad(v, g, q):
        upstream = g[...].reshape(rows, lanes)
        low, high = [
            lax.dot_general(v[q, h:h + pairs].reshape(rows, lanes), upstream, (((0,), (0,)), ((), ())), preferred_element_type=F32)
            for h in range(2)
        ]
        return jnp.concatenate([
            low[:chan, :chan] + low[chan:, chan:],
            low[chan:, :chan] + high[:chan, chan:],
            high[:chan, :chan] + high[chan:, chan:],
        ], axis=0)

    def put_pair(first, second):
        first, second = first.astype(BF16), second.astype(BF16)
        for s in range(2):
            cut = slice(s * chan, (s + 1) * chan)
            gpair[:, :, 2 * s * chan:(2 * s + 1) * chan] = first[:, :, cut]
            gpair[:, :, (2 * s + 1) * chan:(2 * s + 2) * chan] = second[:, :, cut]

    def pair_grad(v, q):
        def row(t):
            return v[q, t // 2:t // 2 + pairs, :, (t % 2) * chan:(t % 2 + 1) * chan].reshape(rows, chan)

        upstream = jnp.concatenate([gpair[:, :, :lanes].reshape(rows, lanes), gpair[:, :, lanes:].reshape(rows, lanes)], axis=0)
        taps = jnp.concatenate([jnp.concatenate([row(p), row(p + 1)], axis=0) for p in range(3)], axis=1)
        both = lax.dot_general(taps, upstream, (((0,), (0,)), ((), ())), preferred_element_type=F32)
        return both[:, :chan], both[:, chan:]

    def stage(kind, q, value):
        wsend[kind, 0, q] = value[:half].astype(BF16)
        wsend[kind, 1, q] = value[half:].astype(BF16)

    def core_send(kind, q=None):
        cut = (slice(None),) if q is None else (q,)
        copy = to_device(wsend.at[(kind, 1 - core) + cut], crecv.at[(kind,) + cut], new_sem(), new_sem(), sibling)
        copy.start()
        flying["core", kind, q] = copy.wait_recv
        flying["core out", kind, q] = copy.wait_send

    def at_places(act, rest=None):
        pl.when(is_place)(act)
        if rest is not None and n_place < plane:
            pl.when(jnp.logical_not(is_place))(rest)

    my_place_or_none = jnp.where(is_place, my_place, n_place)

    def cut_of(q):
        return (pl.ds(0, 3), range(3)) if q is None else (q, (q,))

    def plane_send(kind, q=None):
        settle("core", kind, q)
        cut, qs = cut_of(q)
        for t in qs:
            both = wsend[kind, core, t].astype(F32) + crecv[kind, t].astype(F32)
            rsrc[kind, t] = both.astype(BF16).reshape(n_place, part_rows, chan)
        send, recv = new_sem(), new_sem()
        for t in range(n_place):
            @pl.when(my_place_or_none != t)
            def _():
                to_device(rsrc.at[kind, cut, t], prec.at[kind, my_place, cut], send, recv, (my_lon, t * 2 + core)).start()

        def keep():
            for t in qs:
                prec[kind, pl.ds(my_place, 1), t] = rsrc[kind, t, pl.ds(my_place, 1)]

        at_places(keep)
        flying["plane out", kind, q] = lambda: at_places(
            lambda: wait_bytes(rsrc.at[kind, cut, pl.ds(0, n_place - 1)], send),
            lambda: wait_bytes(rsrc.at[kind, cut], send))
        flying["plane", kind, q] = lambda: at_places(lambda: wait_bytes(prec.at[kind, pl.ds(0, plane - 1), cut], recv))

    def plane_sum(kind, q):
        return jnp.sum(prec[kind, :, q].astype(F32), axis=0)

    def band_send(kind, q, value):
        settle("plane", kind, q)
        cut, qs = cut_of(q)
        send, recv = new_sem(), new_sem()

        def start():
            for t in qs:
                zrec[kind, pl.ds(my_lon, 1), t] = value(t).astype(BF16)[None]
            piece = zrec.at[kind, my_lon, cut]
            for band in bands:
                to_device(piece, piece, send, recv, (band, my_batch)).start()

        at_places(start)
        slots = zrec.at[kind, pl.ds(0, n_lon - 1), cut]
        flying["band out", kind, q] = lambda: at_places(lambda: wait_bytes(slots, send))
        flying["band", kind, q] = lambda: at_places(lambda: wait_bytes(slots, recv))

    def band_sum(kind, q):
        return jnp.sum(zrec[kind, :, q].astype(F32), axis=0)

    def spread_plane(which, q, value):
        cut, qs = cut_of(q)
        send, recv = new_sem(), new_sem()

        def start():
            for t in qs:
                ag[which, core, t, pl.ds(my_place, 1)] = value(t).astype(BF16)[None]
            piece = ag.at[which, core, cut, my_place]
            for k in range(1, plane):
                to_device(piece, piece, send, recv, (my_lon, ((my_place + k) % plane) * 2 + core)).start()

        at_places(start)
        flying["spread out", which, q] = lambda: at_places(lambda: wait_bytes(prec.at[0, pl.ds(0, plane - 1), cut], send))
        flying["spread", which, q] = lambda: at_places(
            lambda: wait_bytes(ag.at[which, core, cut, pl.ds(0, n_place - 1)], recv),
            lambda: wait_bytes(ag.at[which, core, cut], recv))

    def forward_send(which, q=None):
        settle("spread", which, q)
        piece = ag.at[which, core, cut_of(q)[0]]
        copy = to_device(piece, piece, new_sem(), new_sem(), sibling)
        copy.start()
        flying["forward", which, q] = copy.wait_recv
        flying["forward out", which, q] = copy.wait_send

    def finish(which, q, out):
        value = ag[which, :, q].astype(F32).reshape(3 * chan, chan)
        for p in range(3):
            out[pl.ds((p * 3 + q) * chan, chan)] = value[p * chan:(p + 1) * chan]

    def share(index, buf, rows_to_send):
        buf[pl.ds(me, 1)] = jnp.concatenate(rows_to_send, axis=-1)[None]
        send, recv = new_sem(), new_sem()
        for where in others:
            to_device(buf.at[me], buf.at[me], send, recv, where).start()
        slots = buf.at[pl.ds(0, n_dev - 1)]
        flying["share out", index] = lambda: wait_bytes(slots, send)
        flying["share", index] = lambda: wait_bytes(slots, recv)

    def shared(index, buf):
        settle("share", index)
        return [buf[:, :, i * chan:(i + 1) * chan] for i in range(buf.shape[2] // chan)]

    def fold(field):
        both = jnp.sum(field, axis=(0, 1), keepdims=True)[0]
        return both[:, :chan] + both[:, chan:]

    def over_devices(part):
        return jnp.sum(part, axis=0)

    def moments(act):
        sums = fold(act)
        mean = sums * (1.0 / local)
        dev = act - twice(mean)[None]
        return sums, mean, fold(dev * dev), dev

    def merged(sums, squares):
        mean = over_devices(sums) * (1.0 / total)
        off = sums * (1.0 / local) - mean[None]
        var = (over_devices(squares) + local * over_devices(off * off)) * (1.0 / total)
        return mean, lax.rsqrt(var + 1e-05), off

    def wide(row):
        return twice(row)[None]

    settle("load", "x")
    pl.semaphore_wait(barrier, n_dev - 1)
    halo_send(H_X, xin[:, 0], xin[:, width - 1])

    pack_inner(vx, xin[...].reshape(pairs, cells, lanes))
    clear_pads(vx)
    settle("load", "w1")
    kernel_blocks(kc1, kd1, w1f)
    conv_inner(z1, vx, kc1)
    settle("load", "cot")
    sum_cot = fold(cot[...].reshape(pairs, cells, lanes))
    settle("load", "par")
    pack_edges(vx, xin[:, 0], xin[:, width - 1], *halo_get(H_X))
    conv_edges(z1, vx, kc1)

    pre = z1[...] + wide(param(B1))
    act, slope = silu_parts(pre)
    a1[...] = act
    slope1[...] = slope
    sums, mine1, squares, dev = moments(a1[...])
    share(1, ar1, [sums, squares, sum_cot])
    halo_send(H_Z1, *[edge + wide(param(B1)) for edge in first_last(z1)])
    halo_send(H_COT, cot[:, 0], cot[:, width - 1])

    clear_pads(vn)
    clear_pads(vp)
    settle("load", "w2")
    kernel_blocks(kc2, kd2, w2f)
    put_pair(slope1[...], slope1[...] * dev)
    for q in range(3):
        parts[0, q], parts[1, q] = pair_grad(vx, q)
        stage(R_B, q, parts[0, q])
    core_send(R_B)
    plane_send(R_B)

    sums1, squares1, cot_sums = shared(1, ar1)
    shift_two = over_devices(cot_sums)
    cot_mean = shift_two * (1.0 / total)
    mean1, inv1, _ = merged(sums1, squares1)
    off1 = mine1 - mean1
    scale1 = param(G1) * inv1
    shift1 = param(S1) - mean1 * scale1

    def norm_one(a):
        return a * wide(scale1) + wide(shift1)

    pack_inner(vn, norm_one(a1[...]))
    conv_inner(z2, vn, kc2)
    z1_halo = halo_get(H_Z1)
    pack_edges(vn, *[norm_one(a) for a in first_last(a1)], *[norm_one(silu_parts(z)[0]) for z in z1_halo])
    conv_edges(z2, vn, kc2)
    act, slope = silu_parts(z2[...] + wide(param(B2)))
    a2[...] = act
    slope2[...] = slope
    sums, mine2, squares, dev = moments(a2[...])
    c = cot[...].reshape(pairs, cells, lanes) - wide(cot_mean)
    share(2, ar2, [sums, squares, fold(c * dev)])
    halo_send(H_Z2, *[edge + wide(param(B2)) for edge in first_last(z2)])

    def xhat_one(a):
        return (a - wide(mean1)) * wide(inv1)

    for q in range(3):
        stage(R_C, q, inv1 * (parts[1, q] + off1 * parts[0, q]))
    core_send(R_C)
    slope = slope2[...]
    cross, weighed = slope * c, slope * dev
    terms = [fold(cross), fold(weighed), fold(slope)]
    put_pair(cross, weighed)
    for q in range(3):
        parts[0, q], parts[1, q] = pair_grad(vn, q)
    plane_send(R_C)
    gbuf[...] = slope.astype(BF16)
    for q in range(3):
        parts[2, q] = kernel_grad(vn, gbuf, q)

    sums2, squares2, cross2 = shared(2, ar2)
    mean2, inv2, apart2 = merged(sums2, squares2)
    centred = cot_sums - local * cot_mean[None]
    gain_two = inv2 * (over_devices(cross2) + over_devices(apart2 * centred))
    lead2 = param(G2) * inv2
    tilt2 = inv2 * gain_two * (1.0 / total)
    off2 = mine2 - mean2

    def joined(cross, weighed, plain):
        return lead2 * (cross - tilt2 * (weighed + off2 * plain))

    for q in range(3):
        stage(R_W2, q, joined(parts[0, q], parts[1, q], parts[2, q]))
    core_send(R_W2)
    sum_ptg = joined(*terms)

    def pre_two_grad(a, slope, c):
        return wide(lead2) * (c - wide(cot_mean) - (a - wide(mean2)) * wide(tilt2)) * slope

    grad = pre_two_grad(a2[...], slope2[...], cot[...].reshape(pairs, cells, lanes))
    pack_inner(vp, grad)
    conv_inner(dref, vp, kd2)
    plane_send(R_W2)
    grads = []
    for z, ch in zip(halo_get(H_Z2), halo_get(H_COT)):
        a, slope = silu_parts(z)
        grads.append(pre_two_grad(a, slope, ch))
    pack_edges(vp, *first_last(grad), *grads)
    conv_edges(dref, vp, kd2)
    d = dref[...]
    share(3, ar3, [fold(d), fold(d * xhat_one(a1[...])), sum_ptg])
    halo_send(H_D, *first_last(dref))

    scaled = dref[...] * slope1[...]
    gbuf[...] = scaled.astype(BF16)
    for q in range(3):
        stage(R_A, q, kernel_grad(vx, gbuf, q))
    for q in range(3):
        core_send(R_A, q)
    for q in range(3):
        plane_send(R_A, q)
    xhat2 = (a2[...] - wide(mean2)) * wide(inv2)
    y_ref[...] = (xin[...].reshape(pairs, cells, lanes) + xhat2 * wide(param(G2)) + wide(param(S2))).reshape(y_ref.shape)
    band_send(R_W2, None, lambda q: plane_sum(R_W2, q))
    shift_one, gain_one, bias_two = [over_devices(part) for part in shared(3, ar3)]
    lead1 = param(G1) * inv1
    shift_mean, gain_mean = shift_one * (1.0 / total), gain_one * (1.0 / total)
    settle("plane", R_B, None)
    settle("plane", R_C, None)
    for q in range(3):
        band_send(R_A, q, lambda q: lead1 * (plane_sum(R_A, q) - shift_mean * plane_sum(R_B, q) - gain_mean * plane_sum(R_C, q)))

    def pre_one_grad(a, slope, d):
        return wide(lead1) * (d - wide(shift_mean) - xhat_one(a) * wide(gain_mean)) * slope

    grad = pre_one_grad(a1[...], slope1[...], dref[...])
    share(4, ar4, [fold(grad)])
    pack_inner(vp, grad)
    conv_inner(z1, vp, kd1)
    grads = []
    for z, dh in zip(z1_halo, halo_get(H_D)):
        a, slope = silu_parts(z)
        grads.append(pre_one_grad(a, slope, dh))
    pack_edges(vp, *first_last(grad), *grads)
    conv_edges(z1, vp, kd1)
    ig_ref[...] = (cot[...].reshape(pairs, cells, lanes) + z1[...]).reshape(ig_ref.shape)

    settle("band", R_W2, None)
    spread_plane(1, None, lambda q: band_sum(R_W2, q))
    for q in range(3):
        settle("band", R_A, q)
        spread_plane(0, q, lambda q: band_sum(R_A, q))

    forward_send(1)
    for q in range(3):
        forward_send(0, q)
    (bias_one,) = [over_devices(part) for part in shared(4, ar4)]
    for i, row in enumerate((bias_one, gain_one, shift_one, bias_two, gain_two, shift_two)):
        vec_ref[i] = row
    settle("forward", 1, None)
    for q in range(3):
        finish(1, q, wg2_ref)
    for q in range(3):
        settle("forward", 0, q)
        finish(0, q, wg1_ref)

    for key in list(flying):
        settle(*key)


def write_kernel(y, ig, wg1, wg2, vec, y_hbm, ig_hbm, wg1_hbm, wg2_hbm, r0, r1, r2, r3, r4, r5, sem):
    samples, chan = y.shape[2], vec.shape[2]
    copies = []
    for i, (src, dst) in enumerate(((y, y_hbm), (ig, ig_hbm))):
        copies += [
            pltpu.make_async_copy(src.at[:, :, b, pl.ds(s * chan, chan)], dst.at[b, :, s], sem.at[i])
            for b in range(samples)
            for s in range(2)
        ]
    copies += [pltpu.make_async_copy(wg1, wg1_hbm, sem.at[2]), pltpu.make_async_copy(wg2, wg2_hbm, sem.at[3])]
    copies += [pltpu.make_async_copy(vec.at[i], row, sem.at[4 + i]) for i, row in enumerate((r0, r1, r2, r3, r4, r5))]
    for copy in copies:
        copy.start()
    for i, (src, dst) in enumerate(((y, y_hbm), (ig, ig_hbm))):
        pltpu.make_async_copy(src, src, sem.at[i]).wait()
    for copy in copies[-8:]:
        copy.wait()


def on_device(n_lon, n_batch, inputs, weight_one, bias_one, first_norm_scale, first_norm_bias, weight_two, bias_two,
              second_norm_scale, second_norm_bias, cotangent):
    samples, lat, width, chan = inputs.shape
    pairs, cells, lanes = lat // 2, width * samples, 2 * chan
    n_dev = n_lon * n_batch
    half = 3 * chan // 2
    n_place = places_of(n_batch // 2, half // 16)
    part_rows = half // n_place
    field = (pairs, width, samples, lanes)
    flat = (pairs, cells, lanes)
    split = (samples, pairs, 2, width, chan)
    hbm = pl.BlockSpec(memory_space=pltpu.HBM)
    vmem = pl.BlockSpec(memory_space=VMEM)

    shifted = VMEM((3, pairs + 1, cells, lanes), BF16)
    blocks = VMEM((3, 2, lanes, lanes), BF16)
    scratch = [
        VMEM(field, F32), VMEM(field, F32), VMEM((9 * chan, chan), F32), VMEM((9 * chan, chan), F32), VMEM((6, 1, chan), F32),
        shifted, shifted, shifted, blocks, blocks, blocks, blocks,
        VMEM(flat, F32), VMEM(flat, F32), VMEM(flat, F32), VMEM(flat, F32), VMEM(flat, F32), VMEM(flat, F32), VMEM(flat, F32),
        VMEM(flat, BF16), VMEM((pairs, cells, 2 * lanes), BF16), VMEM((3, 3, 3 * chan, chan), F32),
        VMEM((5, 2, pairs * samples, lanes), BF16), VMEM((5, 2, pairs * samples, lanes), BF16),
        VMEM((n_dev, 1, 3 * chan), F32), VMEM((n_dev, 1, 3 * chan), F32), VMEM((n_dev, 1, 3 * chan), F32), VMEM((n_dev, 1, chan), F32),
        VMEM((4, 2, 3, half, chan), BF16), VMEM((4, 3, half, chan), BF16), VMEM((4, 3, n_place, part_rows, chan), BF16),
        VMEM((4, n_batch // 2, 3, part_rows, chan), BF16), VMEM((4, n_lon, 3, part_rows, chan), BF16),
        VMEM((2, 2, 3, n_place, part_rows, chan), BF16), DMA((96,)),
    ]
    small = (bias_one, first_norm_scale, first_norm_bias, bias_two, second_norm_scale, second_norm_bias)
    y, ig, wg1, wg2, vec = pl.pallas_call(
        functools.partial(main_kernel, n_lon, n_batch),
        out_shape=(VMEM(field, F32), VMEM(field, F32), VMEM((9 * chan, chan), F32), VMEM((9 * chan, chan), F32), VMEM((6, 1, chan), F32)),
        in_specs=[hbm] * 10,
        out_specs=(vmem,) * 5,
        scratch_shapes=scratch,
        compiler_params=pltpu.CompilerParams(collective_id=0, has_side_effects=True, vmem_limit_bytes=44 * 2**20),
        name="block",
    )(*[
        pltpu.with_memory_space_constraint(v, pltpu.HBM)
        for v in (inputs.reshape(split), cotangent.reshape(split), weight_one.reshape(9 * chan, chan),
                  weight_two.reshape(9 * chan, chan), *[v.reshape(1, chan) for v in small])
    ])
    outs = pl.pallas_call(
        write_kernel,
        out_shape=(jax.ShapeDtypeStruct(split, F32),) * 2 + (jax.ShapeDtypeStruct((9 * chan, chan), F32),) * 2
        + (jax.ShapeDtypeStruct((1, chan), F32),) * 6,
        in_specs=[vmem] * 5,
        out_specs=(hbm,) * 10,
        scratch_shapes=[DMA((10,))],
        name="write",
    )(*[pltpu.with_memory_space_constraint(v, VMEM) for v in (y, ig, wg1, wg2, vec)])
    rows = [v.reshape(chan) for v in outs[4:]]
    return (outs[0].reshape(inputs.shape), outs[1].reshape(inputs.shape), outs[2].reshape(3, 3, chan, chan), rows[0], rows[1], rows[2],
            outs[3].reshape(3, 3, chan, chan), rows[3], rows[4], rows[5])


def solution(mesh):
    wide = P("batch", None, "lon", None)
    return jax.shard_map(
        functools.partial(on_device, mesh.shape["lon"], mesh.shape["batch"]),
        mesh=mesh,
        in_specs=(wide,) + (P(),) * 8 + (wide,),
        out_specs=(wide, wide) + (P(),) * 8,
        check_vma=False,
    )
```

```python
import functools

import jax
import jax.numpy as jnp
from jax import lax
from jax.experimental import pallas as pl
from jax.experimental.pallas import tpu as pltpu
from jax.sharding import PartitionSpec as P

MESH = pl.DeviceIdType.MESH
F32, BF16 = jnp.float32, jnp.bfloat16
VMEM = pltpu.VMEM
DMA = pltpu.SemaphoreType.DMA

H_X, H_COT, H_Z1, H_Z2, H_D = range(5)
R_B, R_C, R_W2, R_A = range(4)
B1, G1, S1, B2, G2, S2 = range(6)


def twice(row):
    return jnp.concatenate([row, row], axis=-1)


def silu(pre):
    return pre * (0.5 * jnp.tanh(0.5 * pre) + 0.5)


def silu_parts(pre):
    sig = 0.5 * jnp.tanh(0.5 * pre) + 0.5
    return pre * sig, sig * (1.0 + pre * (1.0 - sig))


def places_of(plane, tiles):
    return max(d for d in range(1, min(plane, tiles) + 1) if tiles % d == 0)


def main_kernel(n_lon, n_batch, x_hbm, cot_hbm, w1_hbm, w2_hbm, b1_hbm, g1_hbm, s1_hbm, b2_hbm, g2_hbm, s2_hbm,
                y_ref, ig_ref, wg1_ref, wg2_ref, vec_ref,
                xin, cot, w1f, w2f, par, vx, vn, vp, kc1, kc2, kd1, kd2, z1, a1, slope1, z2, a2, slope2, dref, gbuf, gpair, parts,
                hsend, hrecv, ar0, ar1, ar2, ar3, ar4, wsend, crecv, rsrc, prec, zrec, ag, sems):
    samples, pairs, _, width, chan = x_hbm.shape
    lanes, cells = 2 * chan, width * samples
    rows = pairs * cells
    n_dev = n_lon * n_batch
    plane = n_batch // 2
    local = 2.0 * rows
    total = local * n_dev
    half = wsend.shape[3]
    n_place, part_rows = rsrc.shape[2], rsrc.shape[3]

    my_lon, my_batch = lax.axis_index("lon"), lax.axis_index("batch")
    me = my_lon * n_batch + my_batch
    core, my_place = my_batch % 2, my_batch // 2
    is_place = my_place < n_place
    sibling = (my_lon, my_batch + 1 - 2 * core)
    left = ((my_lon + n_lon - 1) % n_lon, my_batch)
    right = ((my_lon + 1) % n_lon, my_batch)

    low = my_lon < n_lon // 2
    bands = []
    for j in range(n_lon - 1):
        down, up = n_lon - 1 - j, j
        bands.append(jnp.where(low, jnp.where(down <= my_lon, down - 1, down), jnp.where(up >= my_lon, up + 1, up)))
    others = [(band, (my_batch + k) % n_batch) for band in bands for k in range(n_batch)]
    others += [(my_lon, (my_batch + k) % n_batch) for k in range(1, n_batch)]

    taken = []

    def new_sem():
        taken.append(0)
        return sems.at[len(taken) - 1]

    def to_device(src, dst, send, recv, where):
        return pltpu.make_async_remote_copy(src, dst, send, recv, device_id=where, device_id_type=MESH)

    def wait_bytes(ref, sem):
        pltpu.make_async_copy(ref, ref, sem).wait()

    flying = {}

    def settle(*key):
        flying.pop(key)()

    inner = 2 * samples

    def field_loads(src, dst, sem):
        return [
            pltpu.make_async_copy(src.at[b, :, s], dst.at[:, :, b, pl.ds(s * chan, chan)], sem)
            for b in range(samples)
            for s in range(2)
        ]

    def load(name, copies, ref, sem):
        for copy in copies:
            copy.start()
        flying["load", name] = functools.partial(wait_bytes, ref, sem)

    sem_x, sem_w1, sem_cot, sem_w2, sem_par = [new_sem() for _ in range(5)]
    load("x", field_loads(x_hbm, xin, sem_x), xin, sem_x)
    load("w1", [pltpu.make_async_copy(w1_hbm, w1f, sem_w1)], w1f, sem_w1)
    load("cot", field_loads(cot_hbm, cot, sem_cot), cot, sem_cot)
    load("w2", [pltpu.make_async_copy(w2_hbm, w2f, sem_w2)], w2f, sem_w2)
    smalls = (b1_hbm, g1_hbm, s1_hbm, b2_hbm, g2_hbm, s2_hbm)
    load("par", [pltpu.make_async_copy(src, par.at[i], sem_par) for i, src in enumerate(smalls)], par, sem_par)

    barrier = pltpu.get_barrier_semaphore()
    for where in others:
        pl.semaphore_signal(barrier, inc=1, device_id=where, device_id_type=MESH)

    def param(i):
        return par[i]

    def column(field, j):
        return field[:, j * samples:(j + 1) * samples, :]

    def halo_send(kind, first, last):
        hsend[kind, 0] = first.reshape(pairs * samples, lanes).astype(BF16)
        hsend[kind, 1] = last.reshape(pairs * samples, lanes).astype(BF16)
        to_west = to_device(hsend.at[kind, 0], hrecv.at[kind, 1], new_sem(), new_sem(), left)
        to_east = to_device(hsend.at[kind, 1], hrecv.at[kind, 0], new_sem(), new_sem(), right)
        pl.when(my_lon == 0)(to_west.start)
        pl.when(my_lon == n_lon - 1)(to_east.start)
        flying["halo out", kind] = lambda: (to_west.wait_send(), to_east.wait_send())
        flying["halo", kind] = lambda: (to_west.wait_recv(), to_east.wait_recv())

        def rest():
            pl.when(my_lon > 0)(to_west.start)
            pl.when(my_lon < n_lon - 1)(to_east.start)

        return rest

    def halo_get(kind):
        settle("halo", kind)
        return [hrecv[kind, side].astype(F32).reshape(pairs, samples, lanes) for side in range(2)]

    def pack_inner(ref, field):
        for s in range(2):
            part = field[:, :, s * chan:(s + 1) * chan]
            rows_at, lanes_at = slice(s, s + pairs), slice((1 - s) * chan, (2 - s) * chan)
            ref[1, rows_at, :, lanes_at] = part.astype(BF16)
            ref[0, rows_at, inner:, lanes_at] = part[:, samples:-samples].astype(BF16)
            ref[2, rows_at, :cells - inner, lanes_at] = part[:, samples:-samples].astype(BF16)

    def pack_edges(ref, first, last, west, east):
        for s in range(2):
            rows_at, lanes_at = slice(s, s + pairs), slice((1 - s) * chan, (2 - s) * chan)
            cut = slice(s * chan, (s + 1) * chan)
            ref[0, rows_at, :inner, lanes_at] = jnp.concatenate([west[:, :, cut], first[:, :, cut]], axis=1).astype(BF16)
            ref[2, rows_at, cells - inner:, lanes_at] = jnp.concatenate([last[:, :, cut], east[:, :, cut]], axis=1).astype(BF16)

    def clear_pads(ref):
        for q in range(3):
            ref[q, 0, :, :chan] = jnp.zeros((cells, chan), BF16)
            ref[q, pairs, :, chan:] = jnp.zeros((cells, chan), BF16)

    def kernel_blocks(forward, backward, weight):
        none = jnp.zeros((chan, chan), BF16)
        for q in range(3):
            taps = [weight[pl.ds((p * 3 + q) * chan, chan), :].astype(BF16) for p in range(3)]
            turned = [tap.T for tap in taps]
            for t in range(4):
                for s in range(2):
                    p = t - s
                    there = 0 <= p <= 2
                    r, c = pl.ds((t % 2) * chan, chan), pl.ds(s * chan, chan)
                    forward[q, t // 2, r, c] = taps[p] if there else none
                    backward[2 - q, t // 2, r, c] = turned[2 - p] if there else none

    def dots(v, blocks, q, lo, hi):
        out = None
        for h in range(2):
            left_side = v[q, h:h + pairs, lo:hi, :].reshape(pairs * (hi - lo), lanes)
            term = jnp.dot(left_side, blocks[q, h], preferred_element_type=F32)
            out = term if out is None else out + term
        return out.reshape(pairs, hi - lo, lanes)

    def conv_inner(out, v, blocks):
        out[...] = dots(v, blocks, 1, 0, cells)
        out[:, inner:, :] += dots(v, blocks, 0, inner, cells)
        out[:, :cells - inner, :] += dots(v, blocks, 2, 0, cells - inner)

    def conv_edges(out, v, blocks):
        out[:, :inner, :] += dots(v, blocks, 0, 0, inner)
        out[:, cells - inner:, :] += dots(v, blocks, 2, cells - inner, cells)

    def first_last(ref):
        return ref[:, :samples, :], ref[:, cells - samples:, :]

    def kernel_grad(v, g, q):
        upstream = g[...].reshape(rows, lanes)
        low, high = [
            lax.dot_general(v[q, h:h + pairs].reshape(rows, lanes), upstream, (((0,), (0,)), ((), ())), preferred_element_type=F32)
            for h in range(2)
        ]
        return jnp.concatenate([
            low[:chan, :chan] + low[chan:, chan:],
            low[chan:, :chan] + high[:chan, chan:],
            high[:chan, :chan] + high[chan:, chan:],
        ], axis=0)

    def put_pair(first, second):
        first, second = first.astype(BF16), second.astype(BF16)
        for s in range(2):
            cut = slice(s * chan, (s + 1) * chan)
            gpair[:, :, 2 * s * chan:(2 * s + 1) * chan] = first[:, :, cut]
            gpair[:, :, (2 * s + 1) * chan:(2 * s + 2) * chan] = second[:, :, cut]

    def pair_grad(v, q):
        def row(t):
            return v[q, t // 2:t // 2 + pairs, :, (t % 2) * chan:(t % 2 + 1) * chan].reshape(rows, chan)

        upstream = jnp.concatenate([gpair[:, :, :lanes].reshape(rows, lanes), gpair[:, :, lanes:].reshape(rows, lanes)], axis=0)
        taps = jnp.concatenate([jnp.concatenate([row(p), row(p + 1)], axis=0) for p in range(3)], axis=1)
        both = lax.dot_general(taps, upstream, (((0,), (0,)), ((), ())), preferred_element_type=F32)
        return both[:, :chan], both[:, chan:]

    def stage(kind, q, value):
        wsend[kind, 0, q] = value[:half].astype(BF16)
        wsend[kind, 1, q] = value[half:].astype(BF16)

    def core_send(kind, q=None):
        cut = (slice(None),) if q is None else (q,)
        copy = to_device(wsend.at[(kind, 1 - core) + cut], crecv.at[(kind,) + cut], new_sem(), new_sem(), sibling)
        copy.start()
        flying["core", kind, q] = copy.wait_recv
        flying["core out", kind, q] = copy.wait_send

    def at_places(act, rest=None):
        pl.when(is_place)(act)
        if rest is not None and n_place < plane:
            pl.when(jnp.logical_not(is_place))(rest)

    my_place_or_none = jnp.where(is_place, my_place, n_place)

    def cut_of(q):
        return (pl.ds(0, 3), range(3)) if q is None else (q, (q,))

    def plane_send(kind, q=None):
        settle("core", kind, q)
        cut, qs = cut_of(q)
        for t in qs:
            both = wsend[kind, core, t].astype(F32) + crecv[kind, t].astype(F32)
            rsrc[kind, t] = both.astype(BF16).reshape(n_place, part_rows, chan)
        send, recv = new_sem(), new_sem()
        for t in range(n_place):
            @pl.when(my_place_or_none != t)
            def _():
                to_device(rsrc.at[kind, cut, t], prec.at[kind, my_place, cut], send, recv, (my_lon, t * 2 + core)).start()

        def keep():
            for t in qs:
                prec[kind, pl.ds(my_place, 1), t] = rsrc[kind, t, pl.ds(my_place, 1)]

        at_places(keep)
        flying["plane out", kind, q] = lambda: at_places(
            lambda: wait_bytes(rsrc.at[kind, cut, pl.ds(0, n_place - 1)], send),
            lambda: wait_bytes(rsrc.at[kind, cut], send))
        flying["plane", kind, q] = lambda: at_places(lambda: wait_bytes(prec.at[kind, pl.ds(0, plane - 1), cut], recv))

    def plane_sum(kind, q):
        return jnp.sum(prec[kind, :, q].astype(F32), axis=0)

    def band_send(kind, q, value):
        settle("plane", kind, q)
        cut, qs = cut_of(q)
        send, recv = new_sem(), new_sem()

        def start():
            for t in qs:
                zrec[kind, pl.ds(my_lon, 1), t] = value(t).astype(BF16)[None]
            piece = zrec.at[kind, my_lon, cut]
            for band in bands:
                to_device(piece, piece, send, recv, (band, my_batch)).start()

        at_places(start)
        slots = zrec.at[kind, pl.ds(0, n_lon - 1), cut]
        flying["band out", kind, q] = lambda: at_places(lambda: wait_bytes(slots, send))
        flying["band", kind, q] = lambda: at_places(lambda: wait_bytes(slots, recv))

    def band_sum(kind, q):
        return jnp.sum(zrec[kind, :, q].astype(F32), axis=0)

    def spread_plane(which, q, value):
        cut, qs = cut_of(q)
        send, recv = new_sem(), new_sem()

        def start():
            for t in qs:
                ag[which, core, t, pl.ds(my_place, 1)] = value(t).astype(BF16)[None]
            piece = ag.at[which, core, cut, my_place]
            for k in range(1, plane):
                to_device(piece, piece, send, recv, (my_lon, ((my_place + k) % plane) * 2 + core)).start()

        at_places(start)
        flying["spread out", which, q] = lambda: at_places(lambda: wait_bytes(prec.at[0, pl.ds(0, plane - 1), cut], send))
        flying["spread", which, q] = lambda: at_places(
            lambda: wait_bytes(ag.at[which, core, cut, pl.ds(0, n_place - 1)], recv),
            lambda: wait_bytes(ag.at[which, core, cut], recv))

    def forward_send(which, q=None):
        settle("spread", which, q)
        piece = ag.at[which, core, cut_of(q)[0]]
        copy = to_device(piece, piece, new_sem(), new_sem(), sibling)
        copy.start()
        flying["forward", which, q] = copy.wait_recv
        flying["forward out", which, q] = copy.wait_send

    def finish(which, q, out):
        value = ag[which, :, q].astype(F32).reshape(3 * chan, chan)
        for p in range(3):
            out[pl.ds((p * 3 + q) * chan, chan)] = value[p * chan:(p + 1) * chan]

    def share(index, buf, rows_to_send):
        buf[pl.ds(me, 1)] = jnp.concatenate(rows_to_send, axis=-1)[None]
        send, recv = new_sem(), new_sem()
        for where in others:
            to_device(buf.at[me], buf.at[me], send, recv, where).start()
        slots = buf.at[pl.ds(0, n_dev - 1)]
        flying["share out", index] = lambda: wait_bytes(slots, send)
        flying["share", index] = lambda: wait_bytes(slots, recv)

    def shared(index, buf):
        settle("share", index)
        return [buf[:, :, i * chan:(i + 1) * chan] for i in range(buf.shape[2] // chan)]

    def fold(field):
        both = jnp.sum(field, axis=(0, 1), keepdims=True)[0]
        return both[:, :chan] + both[:, chan:]

    def over_devices(part):
        return jnp.sum(part, axis=0)

    def moments(act, count):
        sums = fold(act)
        mean = sums * (1.0 / count)
        dev = act - twice(mean)[None]
        return sums, mean, fold(dev * dev), dev

    def merged(sums, squares):
        mean = over_devices(sums) * (1.0 / total)
        off = sums * (1.0 / local) - mean[None]
        var = (over_devices(squares) + local * over_devices(off * off)) * (1.0 / total)
        return mean, lax.rsqrt(var + 1e-05), off

    def wide(row):
        return twice(row)[None]

    settle("load", "x")
    pl.semaphore_wait(barrier, n_dev - 1)
    rest = halo_send(H_X, xin[:, 0], xin[:, width - 1])

    pack_inner(vx, xin[...].reshape(pairs, cells, lanes))
    clear_pads(vx)
    rest()
    settle("load", "w1")
    kernel_blocks(kc1, kd1, w1f)
    conv_inner(z1, vx, kc1)
    settle("load", "cot")
    share(0, ar0, [fold(cot[...].reshape(pairs, cells, lanes))])
    settle("load", "par")

    def first_act(lo, hi):
        act, slope = silu_parts(z1[:, lo:hi, :] + wide(param(B1)))
        a1[:, lo:hi, :] = act
        slope1[:, lo:hi, :] = slope
        return act

    n_edge = 2.0 * pairs * inner
    n_mid = local - 2.0 * n_edge
    mid, mid_mean, mid_squares, _ = moments(first_act(inner, cells - inner), n_mid)
    pack_edges(vx, xin[:, 0], xin[:, width - 1], *halo_get(H_X))
    conv_edges(z1, vx, kc1)

    edge, edge_mean, edge_squares, _ = moments(
        jnp.concatenate([first_act(0, inner), first_act(cells - inner, cells)], axis=1), 2.0 * n_edge)
    apart = mid_mean - edge_mean
    sums, squares = mid + edge, mid_squares + edge_squares + (n_mid * 2.0 * n_edge / local) * apart * apart
    share(1, ar1, [sums, squares])
    rest = halo_send(H_Z1, *[edge + wide(param(B1)) for edge in first_last(z1)])

    clear_pads(vn)
    clear_pads(vp)
    settle("load", "w2")
    kernel_blocks(kc2, kd2, w2f)
    rest()
    halo_send(H_COT, cot[:, 0], cot[:, width - 1])()
    mine1 = sums * (1.0 / local)
    put_pair(slope1[...], slope1[...] * (a1[...] - wide(mine1)))
    for q in range(3):
        parts[0, q], parts[1, q] = pair_grad(vx, q)
        stage(R_B, q, parts[0, q])
    core_send(R_B)
    plane_send(R_B)

    (cot_sums,) = shared(0, ar0)
    sums1, squares1 = shared(1, ar1)
    shift_two = over_devices(cot_sums)
    cot_mean = shift_two * (1.0 / total)
    mean1, inv1, _ = merged(sums1, squares1)
    off1 = mine1 - mean1
    scale1 = param(G1) * inv1
    shift1 = param(S1) - mean1 * scale1

    def norm_one(a):
        return a * wide(scale1) + wide(shift1)

    pack_inner(vn, norm_one(a1[...]))
    conv_inner(z2, vn, kc2)
    z1_halo = halo_get(H_Z1)
    pack_edges(vn, *[norm_one(a) for a in first_last(a1)], *[norm_one(silu_parts(z)[0]) for z in z1_halo])
    conv_edges(z2, vn, kc2)
    a2[...] = silu(z2[...] + wide(param(B2)))
    sums, mine2, squares, dev = moments(a2[...], local)
    c = cot[...].reshape(pairs, cells, lanes) - wide(cot_mean)
    share(2, ar2, [sums, squares, fold(c * dev)])
    rest = halo_send(H_Z2, *[edge + wide(param(B2)) for edge in first_last(z2)])

    def xhat_one(a):
        return (a - wide(mean1)) * wide(inv1)

    for q in range(3):
        stage(R_C, q, inv1 * (parts[1, q] + off1 * parts[0, q]))
    core_send(R_C)
    rest()
    _, slope = silu_parts(z2[...] + wide(param(B2)))
    slope2[...] = slope
    cross, weighed = slope * c, slope * dev
    terms = [fold(cross), fold(weighed), fold(slope)]
    put_pair(cross, weighed)
    for q in range(3):
        parts[0, q], parts[1, q] = pair_grad(vn, q)
    plane_send(R_C)
    gbuf[...] = slope.astype(BF16)
    for q in range(3):
        parts[2, q] = kernel_grad(vn, gbuf, q)

    sums2, squares2, cross2 = shared(2, ar2)
    mean2, inv2, apart2 = merged(sums2, squares2)
    centred = cot_sums - local * cot_mean[None]
    gain_two = inv2 * (over_devices(cross2) + over_devices(apart2 * centred))
    lead2 = param(G2) * inv2
    tilt2 = inv2 * gain_two * (1.0 / total)
    off2 = mine2 - mean2

    def joined(cross, weighed, plain):
        return lead2 * (cross - tilt2 * (weighed + off2 * plain))

    for q in range(3):
        stage(R_W2, q, joined(parts[0, q], parts[1, q], parts[2, q]))
    core_send(R_W2)
    sum_ptg = joined(*terms)

    def pre_two_grad(a, slope, c):
        return wide(lead2) * (c - wide(cot_mean) - (a - wide(mean2)) * wide(tilt2)) * slope

    grad = pre_two_grad(a2[...], slope2[...], cot[...].reshape(pairs, cells, lanes))
    pack_inner(vp, grad)
    conv_inner(dref, vp, kd2)
    plane_send(R_W2)
    grads = []
    for z, ch in zip(halo_get(H_Z2), halo_get(H_COT)):
        a, slope = silu_parts(z)
        grads.append(pre_two_grad(a, slope, ch))
    pack_edges(vp, *first_last(grad), *grads)
    conv_edges(dref, vp, kd2)
    d = dref[...]
    share(3, ar3, [fold(d), fold(d * xhat_one(a1[...]))])
    halo_send(H_D, *first_last(dref))()

    scaled = dref[...] * slope1[...]
    gbuf[...] = scaled.astype(BF16)
    for q in range(3):
        stage(R_A, q, kernel_grad(vx, gbuf, q))
    for q in range(3):
        core_send(R_A, q)
    for q in range(3):
        plane_send(R_A, q)
    xhat2 = (a2[...] - wide(mean2)) * wide(inv2)
    y_ref[...] = (xin[...].reshape(pairs, cells, lanes) + xhat2 * wide(param(G2)) + wide(param(S2))).reshape(y_ref.shape)
    band_send(R_W2, None, lambda q: plane_sum(R_W2, q))
    shift_one, gain_one = [over_devices(part) for part in shared(3, ar3)]
    lead1 = param(G1) * inv1
    shift_mean, gain_mean = shift_one * (1.0 / total), gain_one * (1.0 / total)
    settle("plane", R_B, None)
    settle("plane", R_C, None)
    for q in range(3):
        band_send(R_A, q, lambda q: lead1 * (plane_sum(R_A, q) - shift_mean * plane_sum(R_B, q) - gain_mean * plane_sum(R_C, q)))

    def pre_one_grad(a, slope, d):
        return wide(lead1) * (d - wide(shift_mean) - xhat_one(a) * wide(gain_mean)) * slope

    grad = pre_one_grad(a1[...], slope1[...], dref[...])
    share(4, ar4, [fold(grad), sum_ptg])
    pack_inner(vp, grad)
    conv_inner(z1, vp, kd1)
    grads = []
    for z, dh in zip(z1_halo, halo_get(H_D)):
        a, slope = silu_parts(z)
        grads.append(pre_one_grad(a, slope, dh))
    pack_edges(vp, *first_last(grad), *grads)
    conv_edges(z1, vp, kd1)
    ig_ref[...] = (cot[...].reshape(pairs, cells, lanes) + z1[...]).reshape(ig_ref.shape)

    settle("band", R_W2, None)
    spread_plane(1, None, lambda q: band_sum(R_W2, q))
    for q in range(3):
        settle("band", R_A, q)
        spread_plane(0, q, lambda q: band_sum(R_A, q))

    forward_send(1)
    for q in range(3):
        forward_send(0, q)
    bias_one, bias_two = [over_devices(part) for part in shared(4, ar4)]
    for i, row in enumerate((bias_one, gain_one, shift_one, bias_two, gain_two, shift_two)):
        vec_ref[i] = row
    settle("forward", 1, None)
    for q in range(3):
        finish(1, q, wg2_ref)
    for q in range(3):
        settle("forward", 0, q)
        finish(0, q, wg1_ref)

    for key in list(flying):
        settle(*key)


def write_kernel(y, ig, wg1, wg2, vec, y_hbm, ig_hbm, wg1_hbm, wg2_hbm, r0, r1, r2, r3, r4, r5, sem):
    samples, chan = y.shape[2], vec.shape[2]
    copies = []
    for i, (src, dst) in enumerate(((y, y_hbm), (ig, ig_hbm))):
        copies += [
            pltpu.make_async_copy(src.at[:, :, b, pl.ds(s * chan, chan)], dst.at[b, :, s], sem.at[i])
            for b in range(samples)
            for s in range(2)
        ]
    copies += [pltpu.make_async_copy(wg1, wg1_hbm, sem.at[2]), pltpu.make_async_copy(wg2, wg2_hbm, sem.at[3])]
    copies += [pltpu.make_async_copy(vec.at[i], row, sem.at[4 + i]) for i, row in enumerate((r0, r1, r2, r3, r4, r5))]
    for copy in copies:
        copy.start()
    for i, (src, dst) in enumerate(((y, y_hbm), (ig, ig_hbm))):
        pltpu.make_async_copy(src, src, sem.at[i]).wait()
    for copy in copies[-8:]:
        copy.wait()


def on_device(n_lon, n_batch, inputs, weight_one, bias_one, first_norm_scale, first_norm_bias, weight_two, bias_two,
              second_norm_scale, second_norm_bias, cotangent):
    samples, lat, width, chan = inputs.shape
    pairs, cells, lanes = lat // 2, width * samples, 2 * chan
    n_dev = n_lon * n_batch
    half = 3 * chan // 2
    n_place = places_of(n_batch // 2, half // 16)
    part_rows = half // n_place
    field = (pairs, width, samples, lanes)
    flat = (pairs, cells, lanes)
    split = (samples, pairs, 2, width, chan)
    hbm = pl.BlockSpec(memory_space=pltpu.HBM)
    vmem = pl.BlockSpec(memory_space=VMEM)

    shifted = VMEM((3, pairs + 1, cells, lanes), BF16)
    blocks = VMEM((3, 2, lanes, lanes), BF16)
    scratch = [
        VMEM(field, F32), VMEM(field, F32), VMEM((9 * chan, chan), F32), VMEM((9 * chan, chan), F32), VMEM((6, 1, chan), F32),
        shifted, shifted, shifted, blocks, blocks, blocks, blocks,
        VMEM(flat, F32), VMEM(flat, F32), VMEM(flat, F32), VMEM(flat, F32), VMEM(flat, F32), VMEM(flat, F32), VMEM(flat, F32),
        VMEM(flat, BF16), VMEM((pairs, cells, 2 * lanes), BF16), VMEM((3, 3, 3 * chan, chan), F32),
        VMEM((5, 2, pairs * samples, lanes), BF16), VMEM((5, 2, pairs * samples, lanes), BF16),
        VMEM((n_dev, 1, chan), F32), VMEM((n_dev, 1, 2 * chan), F32), VMEM((n_dev, 1, 3 * chan), F32), VMEM((n_dev, 1, 2 * chan), F32),
        VMEM((n_dev, 1, 2 * chan), F32),
        VMEM((4, 2, 3, half, chan), BF16), VMEM((4, 3, half, chan), BF16), VMEM((4, 3, n_place, part_rows, chan), BF16),
        VMEM((4, n_batch // 2, 3, part_rows, chan), BF16), VMEM((4, n_lon, 3, part_rows, chan), BF16),
        VMEM((2, 2, 3, n_place, part_rows, chan), BF16), DMA((96,)),
    ]
    small = (bias_one, first_norm_scale, first_norm_bias, bias_two, second_norm_scale, second_norm_bias)
    y, ig, wg1, wg2, vec = pl.pallas_call(
        functools.partial(main_kernel, n_lon, n_batch),
        out_shape=(VMEM(field, F32), VMEM(field, F32), VMEM((9 * chan, chan), F32), VMEM((9 * chan, chan), F32), VMEM((6, 1, chan), F32)),
        in_specs=[hbm] * 10,
        out_specs=(vmem,) * 5,
        scratch_shapes=scratch,
        compiler_params=pltpu.CompilerParams(collective_id=0, has_side_effects=True, vmem_limit_bytes=44 * 2**20),
        name="block",
    )(*[
        pltpu.with_memory_space_constraint(v, pltpu.HBM)
        for v in (inputs.reshape(split), cotangent.reshape(split), weight_one.reshape(9 * chan, chan),
                  weight_two.reshape(9 * chan, chan), *[v.reshape(1, chan) for v in small])
    ])
    outs = pl.pallas_call(
        write_kernel,
        out_shape=(jax.ShapeDtypeStruct(split, F32),) * 2 + (jax.ShapeDtypeStruct((9 * chan, chan), F32),) * 2
        + (jax.ShapeDtypeStruct((1, chan), F32),) * 6,
        in_specs=[vmem] * 5,
        out_specs=(hbm,) * 10,
        scratch_shapes=[DMA((10,))],
        name="write",
    )(*[pltpu.with_memory_space_constraint(v, VMEM) for v in (y, ig, wg1, wg2, vec)])
    rows = [v.reshape(chan) for v in outs[4:]]
    return (outs[0].reshape(inputs.shape), outs[1].reshape(inputs.shape), outs[2].reshape(3, 3, chan, chan), rows[0], rows[1], rows[2],
            outs[3].reshape(3, 3, chan, chan), rows[3], rows[4], rows[5])


def solution(mesh):
    wide = P("batch", None, "lon", None)
    return jax.shard_map(
        functools.partial(on_device, mesh.shape["lon"], mesh.shape["batch"]),
        mesh=mesh,
        in_specs=(wide,) + (P(),) * 8 + (wide,),
        out_specs=(wide, wide) + (P(),) * 8,
        check_vma=False,
    )
```

```python
import functools

import jax
import jax.numpy as jnp
from jax import lax
from jax.experimental import pallas as pl
from jax.experimental.pallas import tpu as pltpu
from jax.sharding import PartitionSpec as P

MESH = pl.DeviceIdType.MESH
F32, BF16 = jnp.float32, jnp.bfloat16
VMEM = pltpu.VMEM
DMA = pltpu.SemaphoreType.DMA

H_X, H_COT, H_Z1, H_Z2, H_D = range(5)
R_B, R_C, R_W2, R_A = range(4)
B1, G1, S1, B2, G2, S2 = range(6)


def twice(row):
    return jnp.concatenate([row, row], axis=-1)


def silu(pre):
    return pre * (0.5 * jnp.tanh(0.5 * pre) + 0.5)


def silu_parts(pre):
    sig = 0.5 * jnp.tanh(0.5 * pre) + 0.5
    return pre * sig, sig * (1.0 + pre * (1.0 - sig))


def places_of(plane, tiles):
    return max(d for d in range(1, min(plane, tiles) + 1) if tiles % d == 0)


def main_kernel(n_lon, n_batch, x_hbm, cot_hbm, w1_hbm, w2_hbm, b1_hbm, g1_hbm, s1_hbm, b2_hbm, g2_hbm, s2_hbm,
                y_ref, ig_ref, wg1_ref, wg2_ref, vec_ref,
                xin, cot, w1f, w2f, par, vx, vn, vp, kc1, kc2, kd1, kd2, z1, a1, slope1, z2, a2, slope2, dref, gbuf, gpair, parts,
                hsend, hrecv, ar0, ar1, ar2, ar3, ar4, wsend, crecv, rsrc, prec, zrec, ag, sems):
    samples, pairs, _, width, chan = x_hbm.shape
    lanes, cells = 2 * chan, width * samples
    rows = pairs * cells
    n_dev = n_lon * n_batch
    plane = n_batch // 2
    local = 2.0 * rows
    total = local * n_dev
    half = wsend.shape[3]
    n_place, part_rows = rsrc.shape[2], rsrc.shape[3]

    my_lon, my_batch = lax.axis_index("lon"), lax.axis_index("batch")
    me = my_lon * n_batch + my_batch
    core, my_place = my_batch % 2, my_batch // 2
    is_place = my_place < n_place
    sibling = (my_lon, my_batch + 1 - 2 * core)
    left = ((my_lon + n_lon - 1) % n_lon, my_batch)
    right = ((my_lon + 1) % n_lon, my_batch)

    low = my_lon < n_lon // 2
    bands = []
    for j in range(n_lon - 1):
        down, up = n_lon - 1 - j, j
        bands.append(jnp.where(low, jnp.where(down <= my_lon, down - 1, down), jnp.where(up >= my_lon, up + 1, up)))
    others = [(band, (my_batch + k) % n_batch) for band in bands for k in range(n_batch)]
    others += [(my_lon, (my_batch + k) % n_batch) for k in range(1, n_batch)]

    taken = []

    def new_sem():
        taken.append(0)
        return sems.at[len(taken) - 1]

    def to_device(src, dst, send, recv, where):
        return pltpu.make_async_remote_copy(src, dst, send, recv, device_id=where, device_id_type=MESH)

    def wait_bytes(ref, sem):
        pltpu.make_async_copy(ref, ref, sem).wait()

    flying = {}

    def settle(*key):
        flying.pop(key)()

    inner = 2 * samples

    def field_loads(src, dst, sem):
        return [
            pltpu.make_async_copy(src.at[b, :, s], dst.at[:, :, b, pl.ds(s * chan, chan)], sem)
            for b in range(samples)
            for s in range(2)
        ]

    def load(name, copies, ref, sem):
        for copy in copies:
            copy.start()
        flying["load", name] = functools.partial(wait_bytes, ref, sem)

    barrier = pltpu.get_barrier_semaphore()
    for where in others:
        pl.semaphore_signal(barrier, inc=1, device_id=where, device_id_type=MESH)

    sem_x, sem_w1, sem_cot, sem_w2, sem_par = [new_sem() for _ in range(5)]
    load("x", field_loads(x_hbm, xin, sem_x), xin, sem_x)
    load("w1", [pltpu.make_async_copy(w1_hbm, w1f, sem_w1)], w1f, sem_w1)
    load("cot", field_loads(cot_hbm, cot, sem_cot), cot, sem_cot)
    load("w2", [pltpu.make_async_copy(w2_hbm, w2f, sem_w2)], w2f, sem_w2)
    smalls = (b1_hbm, g1_hbm, s1_hbm, b2_hbm, g2_hbm, s2_hbm)
    load("par", [pltpu.make_async_copy(src, par.at[i], sem_par) for i, src in enumerate(smalls)], par, sem_par)

    def param(i):
        return par[i]

    def column(field, j):
        return field[:, j * samples:(j + 1) * samples, :]

    def halo_send(kind, first, last):
        hsend[kind, 0] = first.reshape(pairs * samples, lanes).astype(BF16)
        hsend[kind, 1] = last.reshape(pairs * samples, lanes).astype(BF16)
        to_west = to_device(hsend.at[kind, 0], hrecv.at[kind, 1], new_sem(), new_sem(), left)
        to_east = to_device(hsend.at[kind, 1], hrecv.at[kind, 0], new_sem(), new_sem(), right)
        pl.when(my_lon == 0)(to_west.start)
        pl.when(my_lon == n_lon - 1)(to_east.start)
        flying["halo out", kind] = lambda: (to_west.wait_send(), to_east.wait_send())
        flying["halo", kind] = lambda: (to_west.wait_recv(), to_east.wait_recv())

        def rest():
            pl.when(my_lon > 0)(to_west.start)
            pl.when(my_lon < n_lon - 1)(to_east.start)

        return rest

    def halo_get(kind):
        settle("halo", kind)
        return [hrecv[kind, side].astype(F32).reshape(pairs, samples, lanes) for side in range(2)]

    def pack_inner(ref, field):
        for s in range(2):
            part = field[:, :, s * chan:(s + 1) * chan]
            rows_at, lanes_at = slice(s, s + pairs), slice((1 - s) * chan, (2 - s) * chan)
            ref[1, rows_at, :, lanes_at] = part.astype(BF16)
            ref[0, rows_at, inner:, lanes_at] = part[:, samples:-samples].astype(BF16)
            ref[2, rows_at, :cells - inner, lanes_at] = part[:, samples:-samples].astype(BF16)

    def pack_edges(ref, first, last, west, east):
        for s in range(2):
            rows_at, lanes_at = slice(s, s + pairs), slice((1 - s) * chan, (2 - s) * chan)
            cut = slice(s * chan, (s + 1) * chan)
            ref[0, rows_at, :inner, lanes_at] = jnp.concatenate([west[:, :, cut], first[:, :, cut]], axis=1).astype(BF16)
            ref[2, rows_at, cells - inner:, lanes_at] = jnp.concatenate([last[:, :, cut], east[:, :, cut]], axis=1).astype(BF16)

    def clear_pads(ref):
        for q in range(3):
            ref[q, 0, :, :chan] = jnp.zeros((cells, chan), BF16)
            ref[q, pairs, :, chan:] = jnp.zeros((cells, chan), BF16)

    def kernel_blocks(forward, backward, weight):
        none = jnp.zeros((chan, chan), BF16)
        for q in range(3):
            taps = [weight[pl.ds((p * 3 + q) * chan, chan), :].astype(BF16) for p in range(3)]
            turned = [tap.T for tap in taps]
            for t in range(4):
                for s in range(2):
                    p = t - s
                    there = 0 <= p <= 2
                    r, c = pl.ds((t % 2) * chan, chan), pl.ds(s * chan, chan)
                    forward[q, t // 2, r, c] = taps[p] if there else none
                    backward[2 - q, t // 2, r, c] = turned[2 - p] if there else none

    def dots(v, blocks, q, lo, hi):
        out = None
        for h in range(2):
            left_side = v[q, h:h + pairs, lo:hi, :].reshape(pairs * (hi - lo), lanes)
            term = jnp.dot(left_side, blocks[q, h], preferred_element_type=F32)
            out = term if out is None else out + term
        return out.reshape(pairs, hi - lo, lanes)

    def conv_inner(out, v, blocks):
        out[...] = dots(v, blocks, 1, 0, cells)
        out[:, inner:, :] += dots(v, blocks, 0, inner, cells)
        out[:, :cells - inner, :] += dots(v, blocks, 2, 0, cells - inner)

    def conv_edges(out, v, blocks):
        out[:, :inner, :] += dots(v, blocks, 0, 0, inner)
        out[:, cells - inner:, :] += dots(v, blocks, 2, cells - inner, cells)

    def first_last(ref):
        return ref[:, :samples, :], ref[:, cells - samples:, :]

    def kernel_grad(v, g, q):
        upstream = g[...].reshape(rows, lanes)
        low, high = [
            lax.dot_general(v[q, h:h + pairs].reshape(rows, lanes), upstream, (((0,), (0,)), ((), ())), preferred_element_type=F32)
            for h in range(2)
        ]
        return jnp.concatenate([
            low[:chan, :chan] + low[chan:, chan:],
            low[chan:, :chan] + high[:chan, chan:],
            high[:chan, :chan] + high[chan:, chan:],
        ], axis=0)

    def put_pair(first, second):
        first, second = first.astype(BF16), second.astype(BF16)
        for s in range(2):
            cut = slice(s * chan, (s + 1) * chan)
            gpair[:, :, 2 * s * chan:(2 * s + 1) * chan] = first[:, :, cut]
            gpair[:, :, (2 * s + 1) * chan:(2 * s + 2) * chan] = second[:, :, cut]

    def pair_grad(v, q):
        def row(t):
            return v[q, t // 2:t // 2 + pairs, :, (t % 2) * chan:(t % 2 + 1) * chan].reshape(rows, chan)

        upstream = jnp.concatenate([gpair[:, :, :lanes].reshape(rows, lanes), gpair[:, :, lanes:].reshape(rows, lanes)], axis=0)
        taps = jnp.concatenate([jnp.concatenate([row(p), row(p + 1)], axis=0) for p in range(3)], axis=1)
        both = lax.dot_general(taps, upstream, (((0,), (0,)), ((), ())), preferred_element_type=F32)
        return both[:, :chan], both[:, chan:]

    def stage(kind, q, value):
        wsend[kind, 0, q] = value[:half].astype(BF16)
        wsend[kind, 1, q] = value[half:].astype(BF16)

    def core_send(kind, q=None):
        cut = (slice(None),) if q is None else (q,)
        copy = to_device(wsend.at[(kind, 1 - core) + cut], crecv.at[(kind,) + cut], new_sem(), new_sem(), sibling)
        copy.start()
        flying["core", kind, q] = copy.wait_recv
        flying["core out", kind, q] = copy.wait_send

    def at_places(act, rest=None):
        pl.when(is_place)(act)
        if rest is not None and n_place < plane:
            pl.when(jnp.logical_not(is_place))(rest)

    my_place_or_none = jnp.where(is_place, my_place, n_place)

    def cut_of(q):
        return (pl.ds(0, 3), range(3)) if q is None else (q, (q,))

    def plane_send(kind, q=None):
        settle("core", kind, q)
        cut, qs = cut_of(q)
        for t in qs:
            both = wsend[kind, core, t].astype(F32) + crecv[kind, t].astype(F32)
            rsrc[kind, t] = both.astype(BF16).reshape(n_place, part_rows, chan)
        send, recv = new_sem(), new_sem()
        for t in range(n_place):
            @pl.when(my_place_or_none != t)
            def _():
                to_device(rsrc.at[kind, cut, t], prec.at[kind, my_place, cut], send, recv, (my_lon, t * 2 + core)).start()

        def keep():
            for t in qs:
                prec[kind, pl.ds(my_place, 1), t] = rsrc[kind, t, pl.ds(my_place, 1)]

        at_places(keep)
        flying["plane out", kind, q] = lambda: at_places(
            lambda: wait_bytes(rsrc.at[kind, cut, pl.ds(0, n_place - 1)], send),
            lambda: wait_bytes(rsrc.at[kind, cut], send))
        flying["plane", kind, q] = lambda: at_places(lambda: wait_bytes(prec.at[kind, pl.ds(0, plane - 1), cut], recv))

    def plane_sum(kind, q):
        return jnp.sum(prec[kind, :, q].astype(F32), axis=0)

    def band_send(kind, q, value):
        settle("plane", kind, q)
        cut, qs = cut_of(q)
        send, recv = new_sem(), new_sem()

        def start():
            for t in qs:
                zrec[kind, pl.ds(my_lon, 1), t] = value(t).astype(BF16)[None]
            piece = zrec.at[kind, my_lon, cut]
            for band in bands:
                to_device(piece, piece, send, recv, (band, my_batch)).start()

        at_places(start)
        slots = zrec.at[kind, pl.ds(0, n_lon - 1), cut]
        flying["band out", kind, q] = lambda: at_places(lambda: wait_bytes(slots, send))
        flying["band", kind, q] = lambda: at_places(lambda: wait_bytes(slots, recv))

    def band_sum(kind, q):
        return jnp.sum(zrec[kind, :, q].astype(F32), axis=0)

    def spread_plane(which, q, value):
        cut, qs = cut_of(q)
        send, recv = new_sem(), new_sem()

        def start():
            for t in qs:
                ag[which, core, t, pl.ds(my_place, 1)] = value(t).astype(BF16)[None]
            piece = ag.at[which, core, cut, my_place]
            for k in range(1, plane):
                to_device(piece, piece, send, recv, (my_lon, ((my_place + k) % plane) * 2 + core)).start()

        at_places(start)
        flying["spread out", which, q] = lambda: at_places(lambda: wait_bytes(prec.at[0, pl.ds(0, plane - 1), cut], send))
        flying["spread", which, q] = lambda: at_places(
            lambda: wait_bytes(ag.at[which, core, cut, pl.ds(0, n_place - 1)], recv),
            lambda: wait_bytes(ag.at[which, core, cut], recv))

    def forward_send(which, q=None):
        settle("spread", which, q)
        piece = ag.at[which, core, cut_of(q)[0]]
        copy = to_device(piece, piece, new_sem(), new_sem(), sibling)
        copy.start()
        flying["forward", which, q] = copy.wait_recv
        flying["forward out", which, q] = copy.wait_send

    def finish(which, q, out):
        value = ag[which, :, q].astype(F32).reshape(3 * chan, chan)
        for p in range(3):
            out[pl.ds((p * 3 + q) * chan, chan)] = value[p * chan:(p + 1) * chan]

    def share(index, buf, rows_to_send):
        buf[pl.ds(me, 1)] = jnp.concatenate(rows_to_send, axis=-1)[None]
        send, recv = new_sem(), new_sem()
        for where in others:
            to_device(buf.at[me], buf.at[me], send, recv, where).start()
        slots = buf.at[pl.ds(0, n_dev - 1)]
        flying["share out", index] = lambda: wait_bytes(slots, send)
        flying["share", index] = lambda: wait_bytes(slots, recv)

    def shared(index, buf):
        settle("share", index)
        return [buf[:, :, i * chan:(i + 1) * chan] for i in range(buf.shape[2] // chan)]

    def fold(field):
        both = jnp.sum(field, axis=(0, 1), keepdims=True)[0]
        return both[:, :chan] + both[:, chan:]

    def over_devices(part):
        return jnp.sum(part, axis=0)

    def moments(act, count):
        sums = fold(act)
        mean = sums * (1.0 / count)
        dev = act - twice(mean)[None]
        return sums, mean, fold(dev * dev), dev

    def merged(sums, squares):
        mean = over_devices(sums) * (1.0 / total)
        off = sums * (1.0 / local) - mean[None]
        var = (over_devices(squares) + local * over_devices(off * off)) * (1.0 / total)
        return mean, lax.rsqrt(var + 1e-05), off

    def wide(row):
        return twice(row)[None]

    settle("load", "x")
    pl.semaphore_wait(barrier, n_dev - 1)
    rest = halo_send(H_X, xin[:, 0], xin[:, width - 1])

    pack_inner(vx, xin[...].reshape(pairs, cells, lanes))
    clear_pads(vx)
    rest()
    settle("load", "w1")
    kernel_blocks(kc1, kd1, w1f)
    conv_inner(z1, vx, kc1)
    settle("load", "cot")
    share(0, ar0, [fold(cot[...].reshape(pairs, cells, lanes))])
    settle("load", "par")

    def first_act(lo, hi):
        act, slope = silu_parts(z1[:, lo:hi, :] + wide(param(B1)))
        a1[:, lo:hi, :] = act
        slope1[:, lo:hi, :] = slope
        return act

    n_edge = 2.0 * pairs * inner
    n_mid = local - 2.0 * n_edge
    mid, mid_mean, mid_squares, _ = moments(first_act(inner, cells - inner), n_mid)
    pack_edges(vx, xin[:, 0], xin[:, width - 1], *halo_get(H_X))
    conv_edges(z1, vx, kc1)

    edge, edge_mean, edge_squares, _ = moments(
        jnp.concatenate([first_act(0, inner), first_act(cells - inner, cells)], axis=1), 2.0 * n_edge)
    apart = mid_mean - edge_mean
    sums, squares = mid + edge, mid_squares + edge_squares + (n_mid * 2.0 * n_edge / local) * apart * apart
    share(1, ar1, [sums, squares])
    rest = halo_send(H_Z1, *[edge + wide(param(B1)) for edge in first_last(z1)])

    clear_pads(vn)
    clear_pads(vp)
    settle("load", "w2")
    kernel_blocks(kc2, kd2, w2f)
    rest()
    halo_send(H_COT, cot[:, 0], cot[:, width - 1])()
    mine1 = sums * (1.0 / local)
    put_pair(slope1[...], slope1[...] * (a1[...] - wide(mine1)))
    for q in range(3):
        parts[0, q], parts[1, q] = pair_grad(vx, q)
        stage(R_B, q, parts[0, q])
    core_send(R_B)
    plane_send(R_B)

    (cot_sums,) = shared(0, ar0)
    sums1, squares1 = shared(1, ar1)
    shift_two = over_devices(cot_sums)
    cot_mean = shift_two * (1.0 / total)
    mean1, inv1, _ = merged(sums1, squares1)
    off1 = mine1 - mean1
    scale1 = param(G1) * inv1
    shift1 = param(S1) - mean1 * scale1

    def norm_one(a):
        return a * wide(scale1) + wide(shift1)

    pack_inner(vn, norm_one(a1[...]))
    conv_inner(z2, vn, kc2)
    z1_halo = halo_get(H_Z1)
    pack_edges(vn, *[norm_one(a) for a in first_last(a1)], *[norm_one(silu_parts(z)[0]) for z in z1_halo])
    conv_edges(z2, vn, kc2)
    a2[...] = silu(z2[...] + wide(param(B2)))
    sums, mine2, squares, dev = moments(a2[...], local)
    c = cot[...].reshape(pairs, cells, lanes) - wide(cot_mean)
    share(2, ar2, [sums, squares, fold(c * dev)])
    rest = halo_send(H_Z2, *[edge + wide(param(B2)) for edge in first_last(z2)])

    def xhat_one(a):
        return (a - wide(mean1)) * wide(inv1)

    for q in range(3):
        stage(R_C, q, inv1 * (parts[1, q] + off1 * parts[0, q]))
    core_send(R_C)
    rest()
    _, slope = silu_parts(z2[...] + wide(param(B2)))
    slope2[...] = slope
    cross, weighed = slope * c, slope * dev
    terms = [fold(cross), fold(weighed), fold(slope)]
    put_pair(cross, weighed)
    for q in range(3):
        parts[0, q], parts[1, q] = pair_grad(vn, q)
    plane_send(R_C)
    gbuf[...] = slope.astype(BF16)
    for q in range(3):
        parts[2, q] = kernel_grad(vn, gbuf, q)

    sums2, squares2, cross2 = shared(2, ar2)
    mean2, inv2, apart2 = merged(sums2, squares2)
    centred = cot_sums - local * cot_mean[None]
    gain_two = inv2 * (over_devices(cross2) + over_devices(apart2 * centred))
    lead2 = param(G2) * inv2
    tilt2 = inv2 * gain_two * (1.0 / total)
    off2 = mine2 - mean2

    def joined(cross, weighed, plain):
        return lead2 * (cross - tilt2 * (weighed + off2 * plain))

    for q in range(3):
        stage(R_W2, q, joined(parts[0, q], parts[1, q], parts[2, q]))
    core_send(R_W2)
    sum_ptg = joined(*terms)

    def pre_two_grad(a, slope, c):
        return wide(lead2) * (c - wide(cot_mean) - (a - wide(mean2)) * wide(tilt2)) * slope

    grad = pre_two_grad(a2[...], slope2[...], cot[...].reshape(pairs, cells, lanes))
    pack_inner(vp, grad)
    conv_inner(dref, vp, kd2)
    plane_send(R_W2)
    grads = []
    for z, ch in zip(halo_get(H_Z2), halo_get(H_COT)):
        a, slope = silu_parts(z)
        grads.append(pre_two_grad(a, slope, ch))
    pack_edges(vp, *first_last(grad), *grads)
    conv_edges(dref, vp, kd2)
    d = dref[...]
    share(3, ar3, [fold(d), fold(d * xhat_one(a1[...]))])
    halo_send(H_D, *first_last(dref))()

    scaled = dref[...] * slope1[...]
    gbuf[...] = scaled.astype(BF16)
    for q in range(3):
        stage(R_A, q, kernel_grad(vx, gbuf, q))
    for q in range(3):
        core_send(R_A, q)
    for q in range(3):
        plane_send(R_A, q)
    xhat2 = (a2[...] - wide(mean2)) * wide(inv2)
    y_ref[...] = (xin[...].reshape(pairs, cells, lanes) + xhat2 * wide(param(G2)) + wide(param(S2))).reshape(y_ref.shape)
    band_send(R_W2, None, lambda q: plane_sum(R_W2, q))
    shift_one, gain_one = [over_devices(part) for part in shared(3, ar3)]
    lead1 = param(G1) * inv1
    shift_mean, gain_mean = shift_one * (1.0 / total), gain_one * (1.0 / total)
    settle("plane", R_B, None)
    settle("plane", R_C, None)
    for q in range(3):
        band_send(R_A, q, lambda q: lead1 * (plane_sum(R_A, q) - shift_mean * plane_sum(R_B, q) - gain_mean * plane_sum(R_C, q)))

    def pre_one_grad(a, slope, d):
        return wide(lead1) * (d - wide(shift_mean) - xhat_one(a) * wide(gain_mean)) * slope

    grad = pre_one_grad(a1[...], slope1[...], dref[...])
    share(4, ar4, [fold(grad), sum_ptg])
    pack_inner(vp, grad)
    conv_inner(z1, vp, kd1)
    grads = []
    for z, dh in zip(z1_halo, halo_get(H_D)):
        a, slope = silu_parts(z)
        grads.append(pre_one_grad(a, slope, dh))
    pack_edges(vp, *first_last(grad), *grads)
    conv_edges(z1, vp, kd1)
    ig_ref[...] = (cot[...].reshape(pairs, cells, lanes) + z1[...]).reshape(ig_ref.shape)

    settle("band", R_W2, None)
    spread_plane(1, None, lambda q: band_sum(R_W2, q))
    for q in range(3):
        settle("band", R_A, q)
        spread_plane(0, q, lambda q: band_sum(R_A, q))

    forward_send(1)
    for q in range(3):
        forward_send(0, q)
    bias_one, bias_two = [over_devices(part) for part in shared(4, ar4)]
    for i, row in enumerate((bias_one, gain_one, shift_one, bias_two, gain_two, shift_two)):
        vec_ref[i] = row
    settle("forward", 1, None)
    for q in range(3):
        finish(1, q, wg2_ref)
    for q in range(3):
        settle("forward", 0, q)
        finish(0, q, wg1_ref)

    for key in list(flying):
        settle(*key)


def write_kernel(y, ig, wg1, wg2, vec, y_hbm, ig_hbm, wg1_hbm, wg2_hbm, r0, r1, r2, r3, r4, r5, sem):
    samples, chan = y.shape[2], vec.shape[2]
    copies = []
    for i, (src, dst) in enumerate(((y, y_hbm), (ig, ig_hbm))):
        copies += [
            pltpu.make_async_copy(src.at[:, :, b, pl.ds(s * chan, chan)], dst.at[b, :, s], sem.at[i])
            for b in range(samples)
            for s in range(2)
        ]
    copies += [pltpu.make_async_copy(wg1, wg1_hbm, sem.at[2]), pltpu.make_async_copy(wg2, wg2_hbm, sem.at[3])]
    copies += [pltpu.make_async_copy(vec.at[i], row, sem.at[4 + i]) for i, row in enumerate((r0, r1, r2, r3, r4, r5))]
    for copy in copies:
        copy.start()
    for i, (src, dst) in enumerate(((y, y_hbm), (ig, ig_hbm))):
        pltpu.make_async_copy(src, src, sem.at[i]).wait()
    for copy in copies[-8:]:
        copy.wait()


def on_device(n_lon, n_batch, inputs, weight_one, bias_one, first_norm_scale, first_norm_bias, weight_two, bias_two,
              second_norm_scale, second_norm_bias, cotangent):
    samples, lat, width, chan = inputs.shape
    pairs, cells, lanes = lat // 2, width * samples, 2 * chan
    n_dev = n_lon * n_batch
    half = 3 * chan // 2
    n_place = places_of(n_batch // 2, half // 16)
    part_rows = half // n_place
    field = (pairs, width, samples, lanes)
    flat = (pairs, cells, lanes)
    split = (samples, pairs, 2, width, chan)
    hbm = pl.BlockSpec(memory_space=pltpu.HBM)
    vmem = pl.BlockSpec(memory_space=VMEM)

    shifted = VMEM((3, pairs + 1, cells, lanes), BF16)
    blocks = VMEM((3, 2, lanes, lanes), BF16)
    scratch = [
        VMEM(field, F32), VMEM(field, F32), VMEM((9 * chan, chan), F32), VMEM((9 * chan, chan), F32), VMEM((6, 1, chan), F32),
        shifted, shifted, shifted, blocks, blocks, blocks, blocks,
        VMEM(flat, F32), VMEM(flat, F32), VMEM(flat, F32), VMEM(flat, F32), VMEM(flat, F32), VMEM(flat, F32), VMEM(flat, F32),
        VMEM(flat, BF16), VMEM((pairs, cells, 2 * lanes), BF16), VMEM((3, 3, 3 * chan, chan), F32),
        VMEM((5, 2, pairs * samples, lanes), BF16), VMEM((5, 2, pairs * samples, lanes), BF16),
        VMEM((n_dev, 1, chan), F32), VMEM((n_dev, 1, 2 * chan), F32), VMEM((n_dev, 1, 3 * chan), F32), VMEM((n_dev, 1, 2 * chan), F32),
        VMEM((n_dev, 1, 2 * chan), F32),
        VMEM((4, 2, 3, half, chan), BF16), VMEM((4, 3, half, chan), BF16), VMEM((4, 3, n_place, part_rows, chan), BF16),
        VMEM((4, n_batch // 2, 3, part_rows, chan), BF16), VMEM((4, n_lon, 3, part_rows, chan), BF16),
        VMEM((2, 2, 3, n_place, part_rows, chan), BF16), DMA((96,)),
    ]
    small = (bias_one, first_norm_scale, first_norm_bias, bias_two, second_norm_scale, second_norm_bias)
    y, ig, wg1, wg2, vec = pl.pallas_call(
        functools.partial(main_kernel, n_lon, n_batch),
        out_shape=(VMEM(field, F32), VMEM(field, F32), VMEM((9 * chan, chan), F32), VMEM((9 * chan, chan), F32), VMEM((6, 1, chan), F32)),
        in_specs=[hbm] * 10,
        out_specs=(vmem,) * 5,
        scratch_shapes=scratch,
        compiler_params=pltpu.CompilerParams(collective_id=0, has_side_effects=True, vmem_limit_bytes=44 * 2**20),
        name="block",
    )(*[
        pltpu.with_memory_space_constraint(v, pltpu.HBM)
        for v in (inputs.reshape(split), cotangent.reshape(split), weight_one.reshape(9 * chan, chan),
                  weight_two.reshape(9 * chan, chan), *[v.reshape(1, chan) for v in small])
    ])
    outs = pl.pallas_call(
        write_kernel,
        out_shape=(jax.ShapeDtypeStruct(split, F32),) * 2 + (jax.ShapeDtypeStruct((9 * chan, chan), F32),) * 2
        + (jax.ShapeDtypeStruct((1, chan), F32),) * 6,
        in_specs=[vmem] * 5,
        out_specs=(hbm,) * 10,
        scratch_shapes=[DMA((10,))],
        name="write",
    )(*[pltpu.with_memory_space_constraint(v, VMEM) for v in (y, ig, wg1, wg2, vec)])
    rows = [v.reshape(chan) for v in outs[4:]]
    return (outs[0].reshape(inputs.shape), outs[1].reshape(inputs.shape), outs[2].reshape(3, 3, chan, chan), rows[0], rows[1], rows[2],
            outs[3].reshape(3, 3, chan, chan), rows[3], rows[4], rows[5])


def solution(mesh):
    wide = P("batch", None, "lon", None)
    return jax.shard_map(
        functools.partial(on_device, mesh.shape["lon"], mesh.shape["batch"]),
        mesh=mesh,
        in_specs=(wide,) + (P(),) * 8 + (wide,),
        out_specs=(wide, wide) + (P(),) * 8,
        check_vma=False,
    )
```
